128 devices in a mesh: gx: 16 (over y, x), yz: 8 (over z, core).
Axes of the slice: x: 4, y: 4, z: 4, core: 2. Of those that a mesh axis runs over, the one named last changes fastest.
Arguments:
- positions: float32 [65536, 384], P(('gx', 'yz')), may hold values from 0 to 4
- vectors: float32 [65536, 768], P(('gx', 'yz')), may hold values from -6 to 6
- send_slots: int32 [128, 128, 4], P(('gx', 'yz')), may hold values from -1 to 511, as said below
- pairs: int32 [32768, 2], P(('gx', 'yz')), may hold values from -1 to 511, as said below
- coarse: int32 [65536], P(('gx', 'yz')), may hold values from 0 to 63
Outputs:
- forces: float32 [65536, 384], P(('gx', 'yz'))
The draws below stay inside these ranges and needn't reach their ends.
Inputs may be any that keep to these rules, and one draw needn't show every extreme that they name: `send_slots`: each (sender, owner) row lists its live slots first and has at most 4 of them; every device sends at least one block to itself; some owner receives 4 blocks from every sender. Each owner's live pairs come first and both entries name live received slots; a -1 row has both entries -1; some owners have 256 live pairs.
All inputs are finite; a program needn't handle non-finite values.
Results may differ from the reference program's by a relative error of at most 0.0003.
Values sent between devices are 32-bit elements; how exact they have to be, the bound alone decides.
A program may use at most 64 MiB of HBM per device.

```python
import math
import jax
import jax.numpy as jnp
from jax import lax

NB = 512
BS = 128
CAP = 4
NP = 256
KC = 64
BLOCKS = 65536
N_GX = 16
N_YZ = 8


def send_counts(key):
    devices = N_GX * N_YZ
    base = jax.random.randint(jax.random.fold_in(key, 101), (devices, devices), 0, CAP + 1)
    full_owner = jax.random.randint(jax.random.fold_in(key, 102), (), 0, devices)
    owner_ids = jnp.arange(devices)
    counts = jnp.where(owner_ids[None, :] == full_owner, CAP, base)
    counts = jnp.where(owner_ids[:, None] == owner_ids[None, :], jnp.maximum(counts, 1), counts)
    return (counts.astype(jnp.int32), full_owner)


def draw_send_slots(key, part):
    counts, full_owner = send_counts(key)
    key = jax.random.fold_in(key, 1)
    devices = N_GX * N_YZ
    chosen = jax.random.randint(key, (devices, devices, CAP), 0, NB)
    slot_ids = jnp.arange(CAP)
    return jnp.where(slot_ids[None, None, :] < counts[:, :, None], chosen, -1).astype(jnp.int32)


def draw_pairs(key, part):
    counts, full_owner = send_counts(key)
    key = jax.random.fold_in(key, 2)
    devices = N_GX * N_YZ
    flat = devices * CAP
    slot_ids = jnp.arange(CAP)
    filled = (slot_ids[None, None, :] < counts.T[:, :, None]).reshape(devices, flat).astype(jnp.int32)
    order = jnp.argsort(1 - filled, axis=1, stable=True)
    total = jnp.sum(filled, axis=1)
    draws_u = jax.random.randint(jax.random.fold_in(key, 3), (devices, NP * 2), 0, 1048576) % total[:, None]
    chosen = jnp.take_along_axis(order, draws_u, axis=1).reshape(devices, NP, 2)
    row_ids = jnp.arange(NP)
    first_pos = 2 * row_ids[None, :] % total[:, None]
    second_pos = (2 * row_ids[None, :] + 1) % total[:, None]
    cover_pair = jnp.stack([jnp.take_along_axis(order, first_pos, axis=1), jnp.take_along_axis(order, second_pos, axis=1)], axis=2)
    cover_rows = (total + 1) // 2
    covering = row_ids[None, :] < cover_rows[:, None]
    chosen = jnp.where(covering[:, :, None], cover_pair, chosen)
    owner_ids = jnp.arange(devices)
    hit_last = (owner_ids[:, None, None] == full_owner) & (row_ids[None, :, None] == NP - 1) & (jnp.arange(2)[None, None, :] == 1)
    chosen = jnp.where(hit_last, flat - 1, chosen)
    live_count = jax.random.randint(jax.random.fold_in(key, 4), (devices,), NP // 2, NP + 1)
    live_count = jnp.minimum(jnp.maximum(live_count, cover_rows), NP)
    heavy = jax.random.permutation(jax.random.fold_in(key, 5), devices)[:3]
    is_heavy = jnp.any(owner_ids[:, None] == heavy[None, :], axis=1) | (owner_ids == full_owner)
    live_count = jnp.where(is_heavy, NP, live_count)
    usable = row_ids[None, :] < live_count[:, None]
    return jnp.where(usable[:, :, None], chosen, -1).reshape(devices * NP, 2).astype(jnp.int32)


def set_ends(result, stream_key, least, largest):
    place = [jax.random.randint(jax.random.fold_in(stream_key, axis), (), 0, length) for axis, length in enumerate(result.shape)]
    main_axis = result.shape.index(max(result.shape))
    next_to = place[:main_axis] + [(place[main_axis] + 1) % result.shape[main_axis]] + place[main_axis + 1:]
    return result.at[tuple(place)].set(least).at[tuple(next_to)].set(largest)


def level_of(rng, extent, shards, low, top_value):
    gain = 1.0
    for position, blocks in shards:
        steps = jax.random.uniform(jax.random.fold_in(jax.random.fold_in(rng, 6), position), (blocks,), jnp.float32, low / len(shards), top_value / len(shards))
        gain = gain * jnp.repeat(jnp.exp(steps), extent[position] // blocks).reshape((-1,) + (1,) * (len(extent) - 1 - position))
    return gain


def bell_draw(stream_key, extent, spread, bound, split=(), held_as=jnp.bfloat16):
    entries = jax.random.normal(stream_key, extent, jnp.float32) * spread
    if len(split) > 0:
        entries = level_of(stream_key, extent, split, -0.22, 0.18) * entries
    return jnp.clip(entries, min=-bound, max=bound).astype(held_as)


def setup_inputs(seed: int = 0) -> dict:
    arg_keys = jax.random.split(jax.random.key(seed), 6)
    positions = jnp.clip(4.0 * jax.random.uniform(arg_keys[0], (BLOCKS, 3 * BS), jnp.float32) ** level_of(arg_keys[0], (BLOCKS, 3 * BS), ((0, 128),), -0.2, 0.2), 0.0, 4.0)
    vectors = bell_draw(arg_keys[1], (BLOCKS, 6 * BS), 1.0, 6.0, ((0, 128),), jnp.float32)
    send_slots = draw_send_slots(jax.random.fold_in(arg_keys[5], 71), 0)
    pairs = draw_pairs(jax.random.fold_in(arg_keys[5], 71), 0)
    coarse = set_ends(jax.random.randint(arg_keys[4], (BLOCKS,), 0, KC), jax.random.fold_in(arg_keys[4], 1), 0, KC - 1).astype(jnp.int32)
    return {"positions": positions, "vectors": vectors, "send_slots": send_slots, "pairs": pairs, "coarse": coarse}


core_sq = 0.25
far_sq = 1.0

def columns(array, count, width):
    return [array[:, index * width:(index + 1) * width] for index in range(count)]

def inner_sum(left, right):
    return sum((left[index][:, :, None] * right[index][:, None, :] for index in range(3)))

def pair_tile(pos_a, vec_a, pos_b, vec_b, factor, width):
    comp_a = columns(pos_a, 3, width)
    comp_b = columns(pos_b, 3, width)
    offsets = [comp_a[index][:, :, None] - comp_b[index][:, None, :] for index in range(3)]
    distance = offsets[0] ** 2 + offsets[1] ** 2 + offsets[2] ** 2 + core_sq
    parts_a = columns(vec_a, 6, width)
    parts_b = columns(vec_b, 6, width)
    line_a, burg_a = (parts_a[0:3], parts_a[3:6])
    line_b, burg_b = (parts_b[0:3], parts_b[3:6])
    coupling = inner_sum(burg_a, burg_b) * inner_sum(line_a, line_b) + 0.5 * inner_sum(burg_a, line_b) * inner_sum(line_a, burg_b)
    weight = coupling * factor / (distance * jnp.sqrt(distance))
    on_a = jnp.concatenate([lax.optimization_barrier(jnp.sum(weight * offsets[index], axis=2)) for index in range(3)], axis=1)
    on_b = jnp.concatenate([-lax.optimization_barrier(jnp.sum(weight * offsets[index], axis=1)) for index in range(3)], axis=1)
    return (on_a, on_b)

def block_moments(vectors, coarse, cells, width):
    parts = columns(vectors, 6, width)
    line, burg = (parts[0:3], parts[3:6])
    per_block = jnp.stack([lax.optimization_barrier(jnp.sum(burg[k_idx] * line[l_idx], axis=1)) for k_idx in range(3) for l_idx in range(3)], axis=1)
    one_hot = (coarse[:, None] == jnp.arange(cells)[None, :]).astype(jnp.float32)
    return jnp.dot(one_hot.T, per_block, precision=lax.Precision.HIGHEST)

def far_tile(pos, vec, moments, width):
    cell_ids = jnp.arange(KC)
    centers = jnp.stack([cell_ids // 16, cell_ids // 4 % 4, cell_ids % 4], axis=1).astype(jnp.float32) + 0.5
    comps = columns(pos, 3, width)
    offsets = [comps[index][:, None, :] - centers[None, :, index, None] for index in range(3)]
    distance = offsets[0] ** 2 + offsets[1] ** 2 + offsets[2] ** 2 + far_sq
    parts = columns(vec, 6, width)
    line, burg = (parts[0:3], parts[3:6])
    strength = sum((burg[k_idx][:, None, :] * moments[None, :, k_idx, l_idx, None] * line[l_idx][:, None, :] for k_idx in range(3) for l_idx in range(3)))
    weight = strength / (math.sqrt(KC) * distance * jnp.sqrt(distance))
    return jnp.concatenate([lax.optimization_barrier(jnp.sum(weight * offsets[index], axis=1)) for index in range(3)], axis=1)

def reference(positions, vectors, send_slots, pairs, coarse):
    devices = N_GX * N_YZ
    global_ids = jnp.arange(devices, dtype=jnp.int32)[:, None, None] * NB + jnp.maximum(send_slots, 0)
    owner_table = jnp.transpose(global_ids, (1, 0, 2)).reshape(devices, devices * CAP)
    pair_rows = jnp.maximum(pairs, 0).reshape(devices, NP * 2)
    pair_ids = jnp.take_along_axis(owner_table, pair_rows, axis=1).reshape(devices * NP, 2).astype(jnp.int32)
    usable = (pairs[:, 0] >= 0).astype(jnp.float32)
    group_size = math.gcd(devices * NP, 64)
    factor = 1.0 / math.sqrt(BS)

    def pair_block(packed):
        ids_group, mask_group = packed
        on_a, on_b = pair_tile(positions[ids_group[:, 0]], vectors[ids_group[:, 0]], positions[ids_group[:, 1]], vectors[ids_group[:, 1]], factor, BS)
        return (on_a * mask_group[:, None], on_b * mask_group[:, None])
    on_a, on_b = lax.map(pair_block, (pair_ids.reshape(-1, group_size, 2), usable.reshape(-1, group_size)))
    near = jax.ops.segment_sum(on_a.reshape(-1, 3 * BS), pair_ids[:, 0], num_segments=BLOCKS)
    near = near + jax.ops.segment_sum(on_b.reshape(-1, 3 * BS), pair_ids[:, 1], num_segments=BLOCKS)
    moments = block_moments(vectors, coarse, KC, BS) / math.sqrt(BLOCKS * BS / KC)
    moments = moments.reshape(KC, 3, 3)
    far_group = math.gcd(BLOCKS, 32)
    far = lax.map(lambda packed: far_tile(packed[0], packed[1], moments, BS), (positions.reshape(-1, far_group, 3 * BS), vectors.reshape(-1, far_group, 6 * BS)))
    return near + far.reshape(BLOCKS, 3 * BS)
```

```python
import math

import jax
import jax.numpy as jnp
from jax import lax
from jax.experimental import pallas as pl
from jax.experimental.pallas import tpu as pltpu
from jax.sharding import PartitionSpec as P

MESH = pl.DeviceIdType.MESH
F32 = jnp.float32
BF16 = jnp.bfloat16
KC = 64
WIDTH = 128
MIDDLE = 2.0
ROWS = 16
UNROLL = 4
VMEM_LIMIT = 50 * 2**20


def high_low(value):
    high = value.astype(BF16)
    return high, (value - high.astype(F32)).astype(BF16)


def features(place, tensor):
    scale = WIDTH**-0.25
    rows = [scale * math.sqrt(1.5) * tensor[k][k] for k in range(3)]
    for k, l in ((0, 1), (0, 2), (1, 2)):
        rows.append(scale * math.sqrt(0.75) * (tensor[k][l] + tensor[l][k]))
        rows.append(scale * 0.5 * (tensor[k][l] - tensor[l][k]))
    square = place[0] * place[0] + place[1] * place[1] + place[2] * place[2] + 0.125
    upper = square.astype(BF16).astype(F32)
    one = jnp.ones_like(square)
    return rows + list(place) + [upper, square - upper, one, one]


def pack_kernel(ids_ref, pos_ref, vec_ref, send_ref, base_ref, packed):
    def group(step, carry):
        rows = pl.ds(pl.multiple_of(step * 8, 8), 8)
        place = [pos_ref[rows, pl.ds(k * WIDTH, WIDTH)] - MIDDLE for k in range(3)]
        line = [vec_ref[rows, pl.ds(k * WIDTH, WIDTH)] for k in range(3)]
        burg = [vec_ref[rows, pl.ds((3 + k) * WIDTH, WIDTH)] for k in range(3)]
        for row, value in enumerate(features(place, [[b * l for l in line] for b in burg])):
            base_ref[pl.ds(step * 8 * ROWS + row, 8, stride=ROWS), :] = value
        square = line[0] * line[0] + line[1] * line[1] + line[2] * line[2]
        inverse = lax.rsqrt(jnp.maximum(square, 1e-36))
        side = jnp.where(line[2] < 0, -inverse, inverse)
        length = square * side
        tilt = 1.0 / (1.0 + line[2] * side)
        out = place + [b * length for b in burg] + [line[0] * side * tilt, line[1] * side * tilt]
        for row, value in enumerate(out):
            packed[pl.ds(step * 64 + row, 8, stride=8), :] = value
        return carry

    lax.fori_loop(0, pos_ref.shape[0] // 8, group, 0)

    def pick(step, carry):
        for part in range(8):
            slot = step * 8 + part
            source = jnp.maximum(ids_ref[slot], 0) * 8
            send_ref[pl.ds(pl.multiple_of(slot * 8, 8), 8), :] = packed[
                pl.ds(pl.multiple_of(source, 8), 8), :
            ]
        return carry

    lax.fori_loop(0, ids_ref.shape[0] // 8, pick, 0)


def moment_kernel(size_gx, size_yz, x_ref, o_ref, near, far, total, send_sem, recv_sem):
    gx, yz = lax.axis_index("gx"), lax.axis_index("yz")
    barrier = pltpu.get_barrier_semaphore()

    def along_yz(step):
        return gx, lax.rem(yz + step, size_yz)

    def along_gx(step):
        return lax.rem(gx + step, size_gx), yz

    for step in range(1, size_yz):
        pl.semaphore_signal(barrier, inc=1, device_id=along_yz(step), device_id_type=MESH)
    for step in range(1, size_gx):
        pl.semaphore_signal(barrier, inc=1, device_id=along_gx(step), device_id_type=MESH)
    pl.semaphore_wait(barrier, size_yz + size_gx - 2)

    def exchange(source, held, other, size, sem):
        copies = [
            pltpu.make_async_remote_copy(
                src_ref=source,
                dst_ref=held.at[step],
                send_sem=send_sem.at[sem + step],
                recv_sem=recv_sem.at[sem + step],
                device_id=other(step),
                device_id_type=MESH,
            )
            for step in range(1, size)
        ]
        for copy in copies:
            copy.start()
        for copy in copies:
            copy.wait()
        result = source[...]
        for step in range(1, size):
            result = result + held[step]
        return result

    total[...] = exchange(x_ref, near, along_yz, size_yz, 0)
    o_ref[...] = exchange(total, far, along_gx, size_gx, size_yz)


def far_kernel(base_ref, left_ref, right_ref, o_ref, tile):
    left = left_ref[...]
    high, low = high_low(left)
    left = jnp.concatenate([high, high, low], axis=1)
    right = right_ref[...].astype(BF16)
    right = jnp.concatenate([right, right], axis=1)

    def pair(step, carry):
        for part in range(4):
            at = step * 8 + part * 2
            first = base_ref[pl.ds(pl.multiple_of(at * ROWS, ROWS), ROWS), :]
            second = base_ref[pl.ds(pl.multiple_of(at * ROWS + ROWS, ROWS), ROWS), :]
            both = jnp.concatenate([first, second], axis=1)
            high, low = high_low(both)
            forms = jnp.dot(
                left, jnp.concatenate([high, low, high], axis=0), preferred_element_type=F32
            )
            root = lax.rsqrt(forms[KC:])
            weight = forms[:KC] * root * (root * root)
            high, low = high_low(weight)
            sums = jnp.dot(
                right, jnp.concatenate([high, low], axis=0), preferred_element_type=F32
            )
            force = both[8:] * sums[6:7] - sums[:8]
            tile[pl.ds(part * 16, 8), :] = force[:, :WIDTH]
            tile[pl.ds(part * 16 + 8, 8), :] = force[:, WIDTH:]
        for k in range(3):
            o_ref[pl.ds(pl.multiple_of(step * 8, 8), 8), pl.ds(k * WIDTH, WIDTH)] = tile[
                pl.ds(1 + k, 8, stride=8), :
            ]
        return carry

    lax.fori_loop(0, o_ref.shape[0] // 8, pair, 0)


def near_kernel(live_ref, pairs_ref, recv_ref, o_ref, base, total):
    slots = o_ref.shape[0]

    def group(step, carry):
        got = [recv_ref[pl.ds(step * 64 + row, 8, stride=8), :] for row in range(8)]
        square = got[6] * got[6] + got[7] * got[7]
        inverse = 1.0 / (1.0 + square)
        line = [2.0 * got[6] * inverse, 2.0 * got[7] * inverse, (1.0 - square) * inverse]
        for row, value in enumerate(
            features(got[:3], [[b * l for l in line] for b in got[3:6]])
        ):
            base[pl.ds(step * 8 * ROWS + row, 8, stride=ROWS), :] = value
        total[pl.ds(pl.multiple_of(step * 64, 64), 64), :] = jnp.zeros((64, WIDTH), F32)
        return carry

    lax.fori_loop(0, slots // 8, group, 0)
    row = lax.broadcasted_iota(jnp.int32, (8, WIDTH), 0)
    zero = jnp.zeros((8, WIDTH), F32)

    def one_pair(first, second):
        tile_a = base[pl.ds(pl.multiple_of(first * ROWS, ROWS), ROWS), :]
        tile_b = base[pl.ds(pl.multiple_of(second * ROWS, ROWS), ROWS), :]
        high_a, low_a = high_low(tile_a)
        left = jnp.concatenate([high_a, high_a, low_a, low_a], axis=0)
        last = tile_b[8:]
        turned = pltpu.roll(last, 2, 0)
        squares = jnp.where(
            row >= 6, turned, jnp.where(row >= 4, 1.0, jnp.where(row >= 1, -2.0 * last, 0.0))
        )
        couplings = jnp.concatenate([tile_b[:8], jnp.where(row == 0, last, 0.0)], axis=0)
        high, low = high_low(
            jnp.concatenate([couplings, jnp.concatenate([zero, squares], axis=0)], axis=1)
        )
        forms = lax.dot_general(
            left,
            jnp.concatenate([high, low, high, low], axis=0),
            (((0,), (0,)), ((), ())),
            preferred_element_type=F32,
        )
        root = lax.rsqrt(forms[:, WIDTH:])
        weight = forms[:, :WIDTH] * root * (root * root)
        high, low = high_low(weight)

        def places(tile):
            value = jnp.concatenate(high_low(tile[8:]), axis=0)
            return jnp.concatenate([value, value], axis=1)

        on_b = jnp.dot(
            places(tile_a), jnp.concatenate([high, low], axis=0), preferred_element_type=F32
        )
        on_a = lax.dot_general(
            places(tile_b),
            jnp.concatenate([high, low], axis=1),
            (((1,), (1,)), ((), ())),
            preferred_element_type=F32,
        )
        return [
            tile[8:] * sums[6:7] - (sums[:8] + sums[8:])
            for tile, sums in ((tile_a, on_a), (tile_b, on_b))
        ]

    def step_pairs(step, carry):
        done = []
        for part in range(UNROLL):
            at = (step * UNROLL + part) * 2
            ids = [pairs_ref[at], pairs_ref[at + 1]]
            forces = one_pair(jnp.maximum(ids[0], 0), jnp.maximum(ids[1], 0))
            done += [(jnp.where(i < 0, slots, i), force) for i, force in zip(ids, forces)]
        for i, force in done:
            place = pl.ds(pl.multiple_of(i * 8, 8), 8)
            total[place, :] = total[place, :] + force
        return carry

    lax.fori_loop(0, (live_ref[0] + UNROLL - 1) // UNROLL, step_pairs, 0)

    def finish(step, carry):
        for k in range(3):
            o_ref[pl.ds(pl.multiple_of(step * 8, 8), 8), pl.ds(k * WIDTH, WIDTH)] = total[
                pl.ds(step * 64 + 1 + k, 8, stride=8), :
            ]
        return carry

    lax.fori_loop(0, slots // 8, finish, 0)


def final_kernel(ids_ref, got_ref, far_ref, o_ref):
    blocks, slots = o_ref.shape[0], got_ref.shape[0]
    high, low = high_low(got_ref[...])
    chunk = 128

    def part(step, carry):
        rows = pl.ds(pl.multiple_of(step * chunk, chunk), chunk)
        index = lax.broadcasted_iota(jnp.int32, (chunk, slots), 0) + step * chunk
        chosen = jnp.where(index == ids_ref[...], 1.0, 0.0).astype(BF16)
        o_ref[rows, :] = (
            far_ref[rows, :]
            + jnp.dot(chosen, high, preferred_element_type=F32)
            + jnp.dot(chosen, low, preferred_element_type=F32)
        )
        return carry

    lax.fori_loop(0, blocks // chunk, part, 0)


VM = pl.BlockSpec(memory_space=pltpu.VMEM)
SM = pl.BlockSpec(memory_space=pltpu.SMEM)


def call(kernel, name, outs, in_specs, scratch, args, cost=None, **params):
    return pl.pallas_call(
        kernel,
        name=name,
        out_shape=outs,
        in_specs=in_specs,
        out_specs=jax.tree.map(lambda _: VM, outs),
        scratch_shapes=scratch,
        cost_estimate=cost,
        compiler_params=pltpu.CompilerParams(vmem_limit_bytes=VMEM_LIMIT, **params),
    )(*args)


def array(*shape):
    return jax.ShapeDtypeStruct(shape, F32)


def far_sides(moments):
    scale = WIDTH**-0.25
    m = moments.reshape(KC, 3, 3)
    rows = [m[:, k, k] / (scale * math.sqrt(1.5)) for k in range(3)]
    for k, l in ((0, 1), (0, 2), (1, 2)):
        rows.append((m[:, k, l] + m[:, l, k]) / (2.0 * scale * math.sqrt(0.75)))
        rows.append((m[:, k, l] - m[:, l, k]) / scale)
    strength = jnp.pad(jnp.stack(rows, axis=1) / math.sqrt(KC), ((0, 0), (0, 7)))
    cell = jnp.arange(KC)
    centers = [(c + (0.5 - MIDDLE)).astype(F32) for c in (cell // 16, cell // 4 % 4, cell % 4)]
    one = jnp.ones((KC,), F32)
    square = sum(c * c for c in centers) + (1.0 - 0.125)
    zero = jnp.zeros((KC,), F32)
    squares = [zero] * 9 + [-2.0 * c for c in centers] + [one, one, square, zero]
    left = jnp.concatenate([strength, jnp.stack(squares, axis=1)], axis=0)
    right = [zero] + centers + [zero, zero, one, zero] + [zero] * 8
    return left, jnp.stack(right, axis=0)


def on_device(positions, vectors, send_slots, pairs, coarse):
    size_gx, size_yz = lax.axis_size("gx"), lax.axis_size("yz")
    devices = size_gx * size_yz
    blocks = positions.shape[0]
    capacity = send_slots.shape[2]
    slots = devices * capacity
    ids = send_slots.reshape(slots)
    axes = ("gx", "yz")

    send, base = call(
        pack_kernel,
        "pack",
        (array(slots * 8, WIDTH), array(blocks * ROWS, WIDTH)),
        [SM, VM, VM],
        [pltpu.VMEM((blocks * 8, WIDTH), F32)],
        (ids, positions, vectors),
    )
    got = lax.all_to_all(
        send.reshape(devices, capacity * 8, WIDTH), axes, split_axis=0, concat_axis=0, tiled=True
    ).reshape(slots * 8, WIDTH)

    parts = [vectors[:, k * WIDTH : (k + 1) * WIDTH] for k in range(6)]
    per_block = jnp.stack(
        [jnp.sum(parts[3 + k] * parts[l], axis=1) for k in range(3) for l in range(3)], axis=1
    )
    one_hot = (coarse[:, None] == jnp.arange(KC)[None, :]).astype(F32)
    local = jnp.dot(one_hot.T, per_block, precision=lax.Precision.HIGHEST)
    local = jnp.pad(local.reshape(KC * 9), (0, 1024 - KC * 9)).reshape(8, WIDTH)
    moments = call(
        lambda *refs: moment_kernel(size_gx, size_yz, *refs),
        "moments",
        array(8, WIDTH),
        [VM],
        [
            pltpu.VMEM((size_yz, 8, WIDTH), F32),
            pltpu.VMEM((size_gx, 8, WIDTH), F32),
            pltpu.VMEM((8, WIDTH), F32),
            pltpu.SemaphoreType.DMA((size_yz + size_gx,)),
            pltpu.SemaphoreType.DMA((size_yz + size_gx,)),
        ],
        (local,),
        collective_id=0,
        has_side_effects=True,
    )
    moments = moments.reshape(1024)[: KC * 9] / math.sqrt(blocks * devices * WIDTH / KC)
    far = call(
        far_kernel,
        "far",
        array(blocks, 3 * WIDTH),
        [VM, VM, VM],
        [pltpu.VMEM((64, WIDTH), F32)],
        (base, *far_sides(moments)),
        cost=pl.CostEstimate(flops=10**9, bytes_accessed=5 * 10**6, transcendentals=4 * 10**6),
    )
    live = jnp.sum((pairs[:, 0] >= 0).astype(jnp.int32)).reshape(1)
    partial_sums = call(
        near_kernel,
        "near",
        array(slots, 3 * WIDTH),
        [SM, SM, VM],
        [pltpu.VMEM((slots * ROWS, WIDTH), F32), pltpu.VMEM((slots * 8 + 8, WIDTH), F32)],
        (live, pairs.reshape(-1), got),
    )
    returned = lax.all_to_all(
        partial_sums.reshape(devices, capacity, 3 * WIDTH),
        axes,
        split_axis=0,
        concat_axis=0,
        tiled=True,
    ).reshape(slots, 3 * WIDTH)
    return call(
        final_kernel,
        "final",
        array(blocks, 3 * WIDTH),
        [VM, VM, VM],
        [],
        (ids.reshape(1, slots), returned, far),
    )


def solution(mesh):
    placed = (
        P(("gx", "yz"), None),
        P(("gx", "yz"), None),
        P(("gx", "yz"), None, None),
        P(("gx", "yz"), None),
        P(("gx", "yz")),
    )
    return jax.shard_map(
        on_device, mesh=mesh, in_specs=placed, out_specs=P(("gx", "yz"), None), check_vma=False
    )
```

```python
import math

import jax
import jax.numpy as jnp
from jax import lax
from jax.experimental import pallas as pl
from jax.experimental.pallas import tpu as pltpu
from jax.sharding import PartitionSpec as P

MESH = pl.DeviceIdType.MESH
F32 = jnp.float32
BF16 = jnp.bfloat16
KC = 64
WIDTH = 128
MIDDLE = 2.0
ROWS = 16
UNROLL = 4
FAR_GROUPS = 1
VMEM_LIMIT = 50 * 2**20


def high_low(value):
    high = value.astype(BF16)
    return high, (value - high.astype(F32)).astype(BF16)


def features(place, tensor):
    scale = WIDTH**-0.25
    rows = [scale * math.sqrt(1.5) * tensor[k][k] for k in range(3)]
    for k, l in ((0, 1), (0, 2), (1, 2)):
        rows.append(scale * math.sqrt(0.75) * (tensor[k][l] + tensor[l][k]))
        rows.append(scale * 0.5 * (tensor[k][l] - tensor[l][k]))
    square = place[0] * place[0] + place[1] * place[1] + place[2] * place[2] + 0.125
    upper = square.astype(BF16).astype(F32)
    one = jnp.ones_like(square)
    return rows + list(place) + [upper, square - upper, one, one]


def pack_kernel(ids_ref, pos_ref, vec_ref, send_ref, base_ref, packed):
    def group(step, carry):
        rows = pl.ds(pl.multiple_of(step * 8, 8), 8)
        place = [pos_ref[rows, pl.ds(k * WIDTH, WIDTH)] - MIDDLE for k in range(3)]
        line = [vec_ref[rows, pl.ds(k * WIDTH, WIDTH)] for k in range(3)]
        burg = [vec_ref[rows, pl.ds((3 + k) * WIDTH, WIDTH)] for k in range(3)]
        for row, value in enumerate(features(place, [[b * l for l in line] for b in burg])):
            base_ref[pl.ds(step * 8 * ROWS + row, 8, stride=ROWS), :] = value
        square = line[0] * line[0] + line[1] * line[1] + line[2] * line[2]
        inverse = lax.rsqrt(jnp.maximum(square, 1e-36))
        side = jnp.where(line[2] < 0, -inverse, inverse)
        length = square * side
        tilt = 1.0 / (1.0 + line[2] * side)
        out = place + [b * length for b in burg] + [line[0] * side * tilt, line[1] * side * tilt]
        for row, value in enumerate(out):
            packed[pl.ds(step * 64 + row, 8, stride=8), :] = value
        return carry

    lax.fori_loop(0, pos_ref.shape[0] // 8, group, 0)

    def pick(step, carry):
        for part in range(8):
            slot = step * 8 + part
            source = jnp.maximum(ids_ref[slot], 0) * 8
            send_ref[pl.ds(pl.multiple_of(slot * 8, 8), 8), :] = packed[
                pl.ds(pl.multiple_of(source, 8), 8), :
            ]
        return carry

    lax.fori_loop(0, ids_ref.shape[0] // 8, pick, 0)


def moment_kernel(size_gx, size_yz, x_ref, o_ref, near, far, total, send_sem, recv_sem):
    gx, yz = lax.axis_index("gx"), lax.axis_index("yz")
    barrier = pltpu.get_barrier_semaphore()

    def along_yz(step):
        return gx, lax.rem(yz + step, size_yz)

    def along_gx(step):
        return lax.rem(gx + step, size_gx), yz

    for step in range(1, size_yz):
        pl.semaphore_signal(barrier, inc=1, device_id=along_yz(step), device_id_type=MESH)
    for step in range(1, size_gx):
        pl.semaphore_signal(barrier, inc=1, device_id=along_gx(step), device_id_type=MESH)
    pl.semaphore_wait(barrier, size_yz + size_gx - 2)

    def exchange(source, held, other, size, sem):
        copies = [
            pltpu.make_async_remote_copy(
                src_ref=source,
                dst_ref=held.at[step],
                send_sem=send_sem.at[sem + step],
                recv_sem=recv_sem.at[sem + step],
                device_id=other(step),
                device_id_type=MESH,
            )
            for step in range(1, size)
        ]
        for copy in copies:
            copy.start()
        for copy in copies:
            copy.wait()
        result = source[...]
        for step in range(1, size):
            result = result + held[step]
        return result

    total[...] = exchange(x_ref, near, along_yz, size_yz, 0)
    o_ref[...] = exchange(total, far, along_gx, size_gx, size_yz)


def far_kernel(pos_ref, base_ref, left_ref, o_ref, *tiles):
    high, low = high_low(left_ref[...])
    left = jnp.concatenate([high, high, low], axis=1)

    def group(step, carry):
        for part in range(FAR_GROUPS):
            far_group(step * FAR_GROUPS + part, left, pos_ref, base_ref, o_ref, tiles[part])
        return carry

    lax.fori_loop(0, o_ref.shape[0] // (8 * FAR_GROUPS), group, 0)


def far_group(step, left, pos_ref, base_ref, o_ref, tile):
    for part in range(4):
        at = (step * 8 + part * 2) * ROWS
        both = jnp.concatenate(
            [base_ref[pl.ds(pl.multiple_of(at + i * ROWS, ROWS), ROWS), :] for i in range(2)], axis=1
        )
        high, low = high_low(both)
        forms = jnp.dot(
            left, jnp.concatenate([high, low, high], axis=0), preferred_element_type=F32
        )
        root = lax.rsqrt(forms[KC:])
        weight = forms[:KC] * root * (root * root)
        w = [weight[8 * v : 8 * v + 8] for v in range(8)]
        s = [w[2 * i] + w[2 * i + 1] for i in range(4)]
        sums = [
            1.5 * (s[3] - s[0]) + 0.5 * (s[2] - s[1]),
            (w[1] + w[3]) + (w[5] + w[7]),
            (s[0] + s[1]) + (s[2] + s[3]),
        ]
        for q, value in enumerate(sums):
            for i in range(2):
                tile[pl.ds(q * 64 + (part * 2 + i) * 8, 8), :] = value[:, i * WIDTH : (i + 1) * WIDTH]
    along_x, upper, t = (
        [tile[pl.ds(q * 64 + r, 8, stride=8), :] for r in range(8)] for q in range(3)
    )
    first = (t[0] + t[1]) + (t[2] + t[3])
    second = (t[4] + t[5]) + (t[6] + t[7])
    whole = first + second
    m = [t[i] + t[i + 4] for i in range(4)]
    centers = [
        sum(along_x[1:], along_x[0]),
        2.0 * sum(upper[1:], upper[0]) - 1.5 * first - 0.5 * second,
        1.5 * (m[3] - m[0]) + 0.5 * (m[2] - m[1]),
    ]
    rows = pl.ds(pl.multiple_of(step * 8, 8), 8)
    for k in range(3):
        column = pl.ds(k * WIDTH, WIDTH)
        o_ref[rows, column] = (pos_ref[rows, column] - MIDDLE) * whole - centers[k]


def near_kernel(live_ref, pairs_ref, recv_ref, o_ref, base, total, *matrices):
    slots = o_ref.shape[0]

    def group(step, carry):
        got = [recv_ref[pl.ds(step * 64 + row, 8, stride=8), :] for row in range(8)]
        square = got[6] * got[6] + got[7] * got[7]
        inverse = 1.0 / (1.0 + square)
        line = [2.0 * got[6] * inverse, 2.0 * got[7] * inverse, (1.0 - square) * inverse]
        for row, value in enumerate(
            features(got[:3], [[b * l for l in line] for b in got[3:6]])
        ):
            base[pl.ds(step * 8 * ROWS + row, 8, stride=ROWS), :] = value
        total[pl.ds(pl.multiple_of(step * 64, 64), 64), :] = jnp.zeros((64, WIDTH), F32)
        return carry

    lax.fori_loop(0, slots // 8, group, 0)
    row = lax.broadcasted_iota(jnp.int32, (8, WIDTH), 0)
    zero = jnp.zeros((8, WIDTH), F32)
    blank = jnp.zeros((ROWS, WIDTH), BF16)

    def ids_of(number):
        at = jnp.maximum(number, 0) * 2
        ids = [jnp.where(number < 0, -1, pairs_ref[at + i]) for i in range(2)]
        return ids, [base[pl.ds(pl.multiple_of(jnp.maximum(i, 0) * ROWS, ROWS), ROWS), :] for i in ids]

    def weights(number):
        _, (tile_a, tile_b) = ids_of(number)
        high_a, low_a = high_low(tile_a)
        left = jnp.concatenate([high_a, high_a, low_a, low_a], axis=0)
        last = tile_b[8:]
        turned = pltpu.roll(last, 2, 0)
        squares = jnp.where(
            row >= 6, turned, jnp.where(row >= 4, 1.0, jnp.where(row >= 1, -2.0 * last, 0.0))
        )
        couplings = jnp.concatenate([tile_b[:8], jnp.where(row == 0, last, 0.0)], axis=0)
        high, low = high_low(
            jnp.concatenate([couplings, jnp.concatenate([zero, squares], axis=0)], axis=1)
        )
        forms = lax.dot_general(
            left,
            jnp.concatenate([high, low, high, low], axis=0),
            (((0,), (0,)), ((), ())),
            preferred_element_type=F32,
        )
        root = lax.rsqrt(forms[:, WIDTH:])
        return high_low(forms[:, :WIDTH] * root * (root * root))

    def places(tile):
        return jnp.concatenate(high_low(tile[8:]), axis=0)

    def two_pairs(number, matrix):
        ids, tiles = zip(*[ids_of(number + i) for i in range(2)])
        value = matrix[...]
        first = [places(tile[0]) for tile in tiles]
        second = [places(tile[1]) for tile in tiles]
        on_b = jnp.dot(
            jnp.concatenate([jnp.concatenate([p, p], axis=1) for p in first], axis=0),
            value,
            preferred_element_type=F32,
        )
        on_a = lax.dot_general(
            jnp.concatenate(
                [
                    jnp.concatenate([second[0], blank], axis=1),
                    jnp.concatenate([blank, second[1]], axis=1),
                ],
                axis=0,
            ),
            value,
            (((1,), (1,)), ((), ())),
            preferred_element_type=F32,
        )
        out = []
        for i in range(2):
            sums = on_a[i * ROWS : (i + 1) * ROWS]
            sums = sums[:, :WIDTH] + sums[:, WIDTH:]
            for side, got in ((0, sums), (1, on_b[i * ROWS : (i + 1) * ROWS, i * WIDTH : (i + 1) * WIDTH])):
                force = tiles[i][side][8:] * got[6:7] - (got[:8] + got[8:])
                out.append((jnp.where(ids[i][side] < 0, slots, ids[i][side]), force))
        return out

    def half(number, fill, drain):
        done = []
        for part in range(UNROLL // 2):
            for i in range(2):
                for k, value in enumerate(weights(number + part * 2 + i)):
                    fill[part][pl.ds(k * WIDTH, WIDTH), pl.ds(i * WIDTH, WIDTH)] = value
            done += two_pairs(number - UNROLL + part * 2, drain[part])
        for i, force in done:
            place = pl.ds(pl.multiple_of(i * 8, 8), 8)
            total[place, :] = total[place, :] + force

    count = UNROLL // 2
    even, odd = matrices[:count], matrices[count:]
    for matrix in matrices:
        matrix[...] = jnp.zeros_like(matrix)

    def step_pairs(step, carry):
        half(step * 2 * UNROLL, even, odd)
        half(step * 2 * UNROLL + UNROLL, odd, even)
        return carry

    lax.fori_loop(0, (live_ref[0] + 3 * UNROLL - 1) // (2 * UNROLL), step_pairs, 0)

    def finish(step, carry):
        for k in range(3):
            o_ref[pl.ds(pl.multiple_of(step * 8, 8), 8), pl.ds(k * WIDTH, WIDTH)] = total[
                pl.ds(step * 64 + 1 + k, 8, stride=8), :
            ]
        return carry

    lax.fori_loop(0, slots // 8, finish, 0)


def final_kernel(ids_ref, got_ref, far_ref, o_ref):
    blocks, slots = o_ref.shape[0], got_ref.shape[0]
    high, low = high_low(got_ref[...])
    chunk = 128

    def part(step, carry):
        rows = pl.ds(pl.multiple_of(step * chunk, chunk), chunk)
        index = lax.broadcasted_iota(jnp.int32, (chunk, slots), 0) + step * chunk
        chosen = jnp.where(index == ids_ref[...], 1.0, 0.0).astype(BF16)
        o_ref[rows, :] = (
            far_ref[rows, :]
            + jnp.dot(chosen, high, preferred_element_type=F32)
            + jnp.dot(chosen, low, preferred_element_type=F32)
        )
        return carry

    lax.fori_loop(0, blocks // chunk, part, 0)


VM = pl.BlockSpec(memory_space=pltpu.VMEM)
SM = pl.BlockSpec(memory_space=pltpu.SMEM)


def call(kernel, name, outs, in_specs, scratch, args, cost=None, **params):
    return pl.pallas_call(
        kernel,
        name=name,
        out_shape=outs,
        in_specs=in_specs,
        out_specs=jax.tree.map(lambda _: VM, outs),
        scratch_shapes=scratch,
        cost_estimate=cost,
        compiler_params=pltpu.CompilerParams(vmem_limit_bytes=VMEM_LIMIT, **params),
    )(*args)


def array(*shape):
    return jax.ShapeDtypeStruct(shape, F32)


def far_sides(moments):
    scale = WIDTH**-0.25
    m = moments.reshape(KC, 3, 3)
    rows = [m[:, k, k] / (scale * math.sqrt(1.5)) for k in range(3)]
    for k, l in ((0, 1), (0, 2), (1, 2)):
        rows.append((m[:, k, l] + m[:, l, k]) / (2.0 * scale * math.sqrt(0.75)))
        rows.append((m[:, k, l] - m[:, l, k]) / scale)
    strength = jnp.pad(jnp.stack(rows, axis=1) / math.sqrt(KC), ((0, 0), (0, 7)))
    cell = jnp.arange(KC)
    centers = [(c + (0.5 - MIDDLE)).astype(F32) for c in (cell // 16, cell // 4 % 4, cell % 4)]
    one = jnp.ones((KC,), F32)
    square = sum(c * c for c in centers) + (1.0 - 0.125)
    zero = jnp.zeros((KC,), F32)
    squares = [zero] * 9 + [-2.0 * c for c in centers] + [one, one, square, zero]
    left = jnp.concatenate([strength, jnp.stack(squares, axis=1)], axis=0)
    return left


def on_device(positions, vectors, send_slots, pairs, coarse):
    size_gx, size_yz = lax.axis_size("gx"), lax.axis_size("yz")
    devices = size_gx * size_yz
    blocks = positions.shape[0]
    capacity = send_slots.shape[2]
    slots = devices * capacity
    ids = send_slots.reshape(slots)
    axes = ("gx", "yz")

    send, base = call(
        pack_kernel,
        "pack",
        (array(slots * 8, WIDTH), array(blocks * ROWS, WIDTH)),
        [SM, VM, VM],
        [pltpu.VMEM((blocks * 8, WIDTH), F32)],
        (ids, positions, vectors),
    )
    got = lax.all_to_all(
        send.reshape(devices, capacity * 8, WIDTH), axes, split_axis=0, concat_axis=0, tiled=True
    ).reshape(slots * 8, WIDTH)

    parts = [vectors[:, k * WIDTH : (k + 1) * WIDTH] for k in range(6)]
    per_block = jnp.stack(
        [jnp.sum(parts[3 + k] * parts[l], axis=1) for k in range(3) for l in range(3)], axis=1
    )
    one_hot = (coarse[:, None] == jnp.arange(KC)[None, :]).astype(F32)
    local = jnp.dot(one_hot.T, per_block, precision=lax.Precision.HIGHEST)
    local = jnp.pad(local.reshape(KC * 9), (0, 1024 - KC * 9)).reshape(8, WIDTH)
    moments = call(
        lambda *refs: moment_kernel(size_gx, size_yz, *refs),
        "moments",
        array(8, WIDTH),
        [VM],
        [
            pltpu.VMEM((size_yz, 8, WIDTH), F32),
            pltpu.VMEM((size_gx, 8, WIDTH), F32),
            pltpu.VMEM((8, WIDTH), F32),
            pltpu.SemaphoreType.DMA((size_yz + size_gx,)),
            pltpu.SemaphoreType.DMA((size_yz + size_gx,)),
        ],
        (local,),
        collective_id=0,
        has_side_effects=True,
    )
    moments = moments.reshape(1024)[: KC * 9] / math.sqrt(blocks * devices * WIDTH / KC)
    far = call(
        far_kernel,
        "far",
        array(blocks, 3 * WIDTH),
        [VM, VM, VM],
        [pltpu.VMEM((192, WIDTH), F32)] * FAR_GROUPS,
        (positions, base, far_sides(moments)),
        cost=pl.CostEstimate(flops=10**9, bytes_accessed=5 * 10**6, transcendentals=4 * 10**6),
    )
    live = jnp.sum((pairs[:, 0] >= 0).astype(jnp.int32)).reshape(1)
    partial_sums = call(
        near_kernel,
        "near",
        array(slots, 3 * WIDTH),
        [SM, SM, VM],
        [pltpu.VMEM((slots * ROWS, WIDTH), F32), pltpu.VMEM((slots * 8 + 8, WIDTH), F32)]
        + [pltpu.VMEM((2 * WIDTH, 2 * WIDTH), BF16)] * UNROLL,
        (live, jnp.pad(pairs, ((0, 3 * UNROLL), (0, 0)), constant_values=-1).reshape(-1), got),
    )
    returned = lax.all_to_all(
        partial_sums.reshape(devices, capacity, 3 * WIDTH),
        axes,
        split_axis=0,
        concat_axis=0,
        tiled=True,
    ).reshape(slots, 3 * WIDTH)
    return call(
        final_kernel,
        "final",
        array(blocks, 3 * WIDTH),
        [VM, VM, VM],
        [],
        (ids.reshape(1, slots), returned, far),
    )


def solution(mesh):
    placed = (
        P(("gx", "yz"), None),
        P(("gx", "yz"), None),
        P(("gx", "yz"), None, None),
        P(("gx", "yz"), None),
        P(("gx", "yz")),
    )
    return jax.shard_map(
        on_device, mesh=mesh, in_specs=placed, out_specs=P(("gx", "yz"), None), check_vma=False
    )
```

```python
import math

import jax
import jax.numpy as jnp
from jax import lax
from jax.experimental import pallas as pl
from jax.experimental.pallas import tpu as pltpu
from jax.sharding import PartitionSpec as P

MESH = pl.DeviceIdType.MESH
F32 = jnp.float32
BF16 = jnp.bfloat16
KC = 64
WIDTH = 128
MIDDLE = 2.0
ROWS = 16
UNROLL = 2
CUBE_UNROLL = 4
CAP = 4
BACK = 12
FAR_GROUPS = 2
LOADS = 8
SIDE_X = 4
VMEM_LIMIT = 60 * 2**20


def high_low(value):
    high = value.astype(BF16)
    return high, (value - high.astype(F32)).astype(BF16)


def couplings(tensor):
    scale = WIDTH**-0.25
    rows = [scale * math.sqrt(1.5) * tensor[k][k] for k in range(3)]
    for k, l in ((0, 1), (0, 2), (1, 2)):
        rows.append(scale * math.sqrt(0.75) * (tensor[k][l] + tensor[l][k]))
        rows.append(scale * 0.5 * (tensor[k][l] - tensor[l][k]))
    return rows


def features(place, tensor):
    square = place[0] * place[0] + place[1] * place[1] + place[2] * place[2] + 0.125
    upper = square.astype(BF16).astype(F32)
    one = jnp.ones_like(square)
    return couplings(tensor) + list(place) + [upper, square - upper, one, one]


def other(step):
    gx, yz = lax.axis_index("gx"), lax.axis_index("yz")
    size_yz = lax.axis_size("yz")
    chips = lax.axis_size("gx") * size_yz // 2
    side_x, side_z = SIDE_X, size_yz // 2
    side_y = lax.axis_size("gx") // side_x
    chip, core = lax.rem(step, chips), step // chips
    first = lax.rem(chip, side_y)
    second = first + lax.rem(chip // side_y, side_x)
    third = second + chip // (side_y * side_x)
    y = lax.rem(gx // side_x + first, side_y)
    x = lax.rem(lax.rem(gx, side_x) + second, side_x)
    z = lax.rem(yz // 2 + third, side_z)
    return y * side_x + x, z * 2 + lax.rem(lax.rem(yz, 2) + core, 2)


def pack_group(step, pos_ref, vec_ref, base_ref, table, packed):
    rows = pl.ds(pl.multiple_of(step * 8, 8), 8)
    place = [pos_ref[rows, pl.ds(k * WIDTH, WIDTH)] - MIDDLE for k in range(3)]
    line = [vec_ref[rows, pl.ds(k * WIDTH, WIDTH)] for k in range(3)]
    burg = [vec_ref[rows, pl.ds((3 + k) * WIDTH, WIDTH)] for k in range(3)]
    for row, value in enumerate(features(place, [[b * l for l in line] for b in burg])):
        base_ref[pl.ds(step * 8 * ROWS + row, 8, stride=ROWS), :] = value
        if row < 9:
            table[rows, pl.ds(row * WIDTH, WIDTH)] = value
    square = line[0] * line[0] + line[1] * line[1] + line[2] * line[2]
    inverse = lax.rsqrt(jnp.maximum(square, 1e-36))
    side = jnp.where(line[2] < 0, -inverse, inverse)
    length = square * side
    tilt = 1.0 / (1.0 + line[2] * side)
    out = place + [b * length for b in burg] + [line[0] * side * tilt, line[1] * side * tilt]
    for row, value in enumerate(out):
        packed[pl.ds(step * 64 + row, 8, stride=8), :] = value


def cell_sums(coarse_ref, table):
    blocks = table.shape[0]
    cells = lax.broadcasted_iota(jnp.int32, (KC, blocks), 0)
    chosen = jnp.where(cells == coarse_ref[...], 1.0, 0.0).astype(BF16)
    parts = []
    for m in range(9):
        high, low = high_low(table[:, m * WIDTH : (m + 1) * WIDTH])
        parts.append(
            jnp.dot(chosen, high, preferred_element_type=F32)
            + jnp.dot(chosen, low, preferred_element_type=F32)
        )
    high, low = high_low(jnp.concatenate(parts, axis=1))
    row = lax.broadcasted_iota(jnp.int32, (ROWS, 9 * WIDTH), 0)
    lane = lax.broadcasted_iota(jnp.int32, (ROWS, 9 * WIDTH), 1)
    along = jnp.where((lane >= row * WIDTH) & (lane < row * WIDTH + WIDTH), 1.0, 0.0).astype(BF16)
    sums = [
        lax.dot_general(along, value, (((1,), (1,)), ((), ())), preferred_element_type=F32)
        for value in (high, low)
    ]
    sums = sums[0] + sums[1]
    return jnp.concatenate([sums[:8], sums[8:]], axis=1)


def far_left(sums, norm):
    row = lax.broadcasted_iota(jnp.int32, (ROWS, KC), 0)
    cell = lax.broadcasted_iota(jnp.int32, (ROWS, KC), 1)
    turned = (row == 4) | (row == 6) | (row == 8)
    square = WIDTH**-0.5
    strength = sums * jnp.where(turned, 2.0 / square * norm, norm / (1.5 * square))
    centers = [(c + (0.5 - MIDDLE)).astype(F32) for c in (cell // 16, cell // 4 % 4, cell % 4)]
    whole = centers[0] * centers[0] + centers[1] * centers[1] + centers[2] * centers[2]
    squares = jnp.where((row == 12) | (row == 13), 1.0, 0.0)
    squares = jnp.where(row == 14, whole + (1.0 - 0.125), squares)
    for k in range(3):
        squares = jnp.where(row == 9 + k, -2.0 * centers[k], squares)
    left = jnp.transpose(jnp.concatenate([strength, squares], axis=1))
    high, low = high_low(left)
    return jnp.concatenate([high, high, low], axis=1)


def stacked(tile):
    return jnp.concatenate(high_low(tile), axis=0)


def beside(first, second):
    blank = jnp.zeros_like(first)
    return jnp.concatenate(
        [jnp.concatenate([first, blank], axis=1), jnp.concatenate([blank, second], axis=1)], axis=0
    )


def forms_of(lefts, rights):
    return lax.dot_general(
        jnp.concatenate(lefts, axis=0),
        beside(*rights),
        (((0,), (0,)), ((), ())),
        preferred_element_type=F32,
    )


def whole_kernel(
    ids_ref,
    pairs_ref,
    id_rows,
    pair_rows,
    coarse_ref,
    pos_hbm,
    vec_hbm,
    o_ref,
    pos_ref,
    vec_ref,
    packed,
    send_ref,
    got_ref,
    base_ref,
    table,
    place_base,
    form_base,
    cubes,
    forces,
    out_ref,
    back_ref,
    mine,
    near,
    total,
    far,
    load_sem,
    send_sem,
    recv_sem,
    bulk_sem,
    round_sem,
    *buffers,
):
    packed_rows, place_rows_ref, form_rows_ref = [
        ref.reshape(ref.shape[0] * ref.shape[1], WIDTH) for ref in (packed, place_base, form_base)
    ]
    tiles, matrices = buffers[:FAR_GROUPS], buffers[FAR_GROUPS:]
    gx, yz = lax.axis_index("gx"), lax.axis_index("yz")
    size_gx, size_yz = lax.axis_size("gx"), lax.axis_size("yz")
    devices = size_gx * size_yz
    me = gx * size_yz + yz
    blocks = pos_ref.shape[0]
    count = pairs_ref.shape[1]
    loaded = blocks // LOADS

    def along_yz(step):
        return gx, lax.rem(yz + step, size_yz)

    def along_gx(step):
        return lax.rem(gx + step, size_gx), yz

    def loads(step):
        rows = pl.ds(pl.multiple_of(step * loaded, loaded), loaded)
        return [
            pltpu.make_async_copy(source.at[rows], target.at[rows], load_sem.at[k, step])
            for k, (source, target) in enumerate(((pos_hbm, pos_ref), (vec_hbm, vec_ref)))
        ]

    barrier = pltpu.get_barrier_semaphore()
    for turn, size in ((along_yz, size_yz), (along_gx, size_gx)):
        for step in range(1, size):
            pl.semaphore_signal(barrier, inc=1, device_id=turn(step), device_id_type=MESH)
    for step in range(LOADS):
        for copy in loads(step):
            copy.start()

    def pack(step, carry):
        for copy in loads(step):
            copy.wait()

        def group(inner, carry):
            pack_group(step * (loaded // 8) + inner, pos_ref, vec_ref, base_ref, table, packed_rows)
            return carry

        return lax.fori_loop(0, loaded // 8, group, carry)

    lax.fori_loop(0, LOADS, pack, 0)
    pl.semaphore_wait(barrier, size_yz + size_gx - 2)
    for step in range(1, size_yz):
        pl.semaphore_signal(round_sem, inc=1, device_id=along_yz(step), device_id_type=MESH)

    def exchange(source, held, turn, size, sem):
        return [
            pltpu.make_async_remote_copy(
                src_ref=source,
                dst_ref=held.at[step],
                send_sem=send_sem.at[sem + step],
                recv_sem=recv_sem.at[sem + step],
                device_id=turn(step),
                device_id_type=MESH,
            )
            for step in range(1, size)
        ]

    def gathered(source, held, copies):
        for copy in copies:
            copy.wait()
        result = source[...]
        for step in range(1, len(copies) + 1):
            result = result + held[step]
        return result

    mine[...] = cell_sums(coarse_ref, table)
    over_yz = exchange(mine, near, along_yz, size_yz, 0)
    over_gx = exchange(total, far, along_gx, size_gx, size_yz)
    for copy in over_yz:
        copy.start()
    pl.semaphore_wait(round_sem, size_yz - 1)

    chunk = CAP * 8
    half = chunk // 2

    def pick(device):
        for slot in range(CAP):
            source = jnp.maximum(ids_ref[slot, device], 0)
            send_ref[pl.ds(device * chunk + slot, 8, stride=CAP), :] = packed[
                source
            ]

    def bulk(step, source, target, pitch, at, size, sem):
        to_gx, to_yz = other(step)
        device = to_gx * size_yz + to_yz
        return pltpu.make_async_remote_copy(
            src_ref=source.at[pl.ds(pl.multiple_of(device * pitch + at, 8), size)],
            dst_ref=target.at[pl.ds(pl.multiple_of(me * pitch + at, 8), size)],
            send_sem=bulk_sem.at[sem],
            recv_sem=bulk_sem.at[sem + 1],
            device_id=(to_gx, to_yz),
            device_id_type=MESH,
        )

    def all_of(source, target, size, sem):
        rows = pl.ds(0, (devices - 1) * size)
        return pltpu.make_async_remote_copy(
            src_ref=source.at[rows],
            dst_ref=target.at[rows],
            send_sem=bulk_sem.at[sem],
            recv_sem=bulk_sem.at[sem + 1],
            device_id=other(1),
            device_id_type=MESH,
        )

    def send_first(step, carry):
        to_gx, to_yz = other(step)
        pick(to_gx * size_yz + to_yz)
        bulk(step, send_ref, got_ref, chunk, 0, half, 0).start()
        return carry

    def send_second(step, carry):
        bulk(step, send_ref, got_ref, chunk, half, half, 2).start()
        return carry

    lax.fori_loop(1, 1 + devices // 4, send_first, 0)
    total[...] = gathered(mine, near, over_yz)
    for copy in over_gx:
        copy.start()
    lax.fori_loop(1 + devices // 4, devices, send_first, 0)
    lax.fori_loop(1, devices, send_second, 0)
    pick(me)
    rows = pl.ds(pl.multiple_of(me * chunk, chunk), chunk)
    got_ref[rows, :] = send_ref[rows, :]
    for matrix in matrices:
        matrix[...] = jnp.zeros_like(matrix)
    form_base[...] = jnp.zeros_like(form_base)

    sums = gathered(total, far, over_gx)
    left = far_left(
        jnp.concatenate([sums[:, :KC], sums[:, KC:]], axis=0),
        1.0 / (math.sqrt(blocks * devices * WIDTH / KC) * math.sqrt(KC)),
    )

    def far_step(step, carry):
        for part in range(FAR_GROUPS):
            far_group(step * FAR_GROUPS + part, left, pos_ref, base_ref, o_ref, tiles[part])
        return carry

    lax.fori_loop(0, blocks // (8 * FAR_GROUPS), far_step, 0)

    def came(step, slot, first, last):
        return [
            got_ref[pl.ds(step * 8 * chunk + CAP * k + slot, 8, stride=chunk), :]
            for k in range(first, last)
        ]

    all_of(send_ref, got_ref, half, 0).wait_recv()

    def place_rows(step, carry):
        for slot in range(CAP):
            place = came(step, slot, 0, 3)
            square = place[0] * place[0] + place[1] * place[1] + place[2] * place[2] + 0.125
            upper = square.astype(BF16).astype(F32)
            one = jnp.ones_like(square)
            values = place + [upper, square - upper, one, one, jnp.zeros_like(square)]
            for row, value in enumerate(values):
                place_rows_ref[pl.ds(step * 64 * CAP + slot * 8 + row, 8, stride=8 * CAP), :] = value
        return carry

    lax.fori_loop(0, devices // 8, place_rows, 0)
    row = lax.broadcasted_iota(jnp.int32, (8, WIDTH), 0)

    def tile_of(base, side, number):
        return base[jnp.maximum(pairs_ref[side, number], 0)]

    def cube_step(step, carry):
        for part in range(CUBE_UNROLL):
            number = (step * CUBE_UNROLL + part) * 2
            lefts, rights = [], []
            for i in range(2):
                value = stacked(tile_of(place_base, 0, number + i))
                lefts += [value, value]
                last = tile_of(place_base, 1, number + i)
                turned = pltpu.roll(last, 2, 0)
                last = jnp.where(
                    row < 3, -2.0 * last, jnp.where(row < 5, 1.0, jnp.where(row < 7, turned, 0.0))
                )
                high, low = high_low(last)
                rights.append(jnp.concatenate([high, high, low, low], axis=0))
            root = lax.rsqrt(forms_of(lefts, rights))
            rows = pl.ds(pl.multiple_of(number * (WIDTH // 2), WIDTH), WIDTH)
            cubes[rows, :] = root * (root * root)
        return carry

    lax.fori_loop(0, count // (2 * CUBE_UNROLL), cube_step, 0)
    all_of(send_ref, got_ref, half, 2).wait_recv()

    def form_rows(step, carry):
        for slot in range(CAP):
            got = came(step, slot, 3, 8)
            square = got[3] * got[3] + got[4] * got[4]
            inverse = 1.0 / (1.0 + square)
            line = [2.0 * got[3] * inverse, 2.0 * got[4] * inverse, (1.0 - square) * inverse]
            for row, value in enumerate(couplings([[b * l for l in line] for b in got[:3]])):
                form_rows_ref[
                    pl.ds(step * 8 * ROWS * CAP + slot * ROWS + row, 8, stride=ROWS * CAP), :
                ] = value
        return carry

    lax.fori_loop(0, devices // 8, form_rows, 0)

    def fill(number, matrix):
        lefts, rights = [], []
        for i in range(2):
            high, low = high_low(tile_of(form_base, 0, number + i))
            lefts += [high, high, low]
            high, low = high_low(tile_of(form_base, 1, number + i))
            rights.append(jnp.concatenate([high, low, high], axis=0))
        rows = pl.ds(pl.multiple_of(number * (WIDTH // 2), WIDTH), WIDTH)
        high, low = high_low(forms_of(lefts, rights) * cubes[rows, :])
        matrix[pl.ds(0, WIDTH), :] = high
        matrix[pl.ds(WIDTH, WIDTH), :] = low

    def drain(number, at, matrix):
        value = matrix[...]
        places = [[tile_of(place_base, side, number + i) for i in range(2)] for side in range(2)]
        first, second = [[stacked(tile) for tile in side] for side in places]
        on_b = jnp.dot(
            jnp.concatenate([jnp.concatenate([p, p], axis=1) for p in first], axis=0),
            value,
            preferred_element_type=F32,
        )
        on_a = lax.dot_general(
            beside(*second), value, (((1,), (1,)), ((), ())), preferred_element_type=F32
        )
        for i in range(2):
            on_first = on_a[i * ROWS : (i + 1) * ROWS]
            on_first = on_first[:, :WIDTH] + on_first[:, WIDTH:]
            on_second = on_b[i * ROWS : (i + 1) * ROWS, i * WIDTH : (i + 1) * WIDTH]
            for side, got in enumerate((on_first, on_second)):
                force = places[side][i] * got[5:6] - (got[:8] + got[8:])
                forces[side, pl.ds(pl.multiple_of((at + i) * 8, 8), 8), :] = force

    even, odd = matrices[:UNROLL], matrices[UNROLL:]

    def half_step(number, filled, drained):
        for part in range(UNROLL):
            fill(jnp.minimum(number + 2 * part, count - 2), filled[part])
            at = number + 2 * part
            before = jnp.clip(at - 2 * UNROLL, 0, count - 2)
            drain(before, at, drained[part])

    def pair_step(step, carry):
        half_step(step * 4 * UNROLL, even, odd)
        half_step(step * 4 * UNROLL + 2 * UNROLL, odd, even)
        return carry

    lax.fori_loop(0, pl.cdiv(count + 2 * UNROLL, 4 * UNROLL), pair_step, 0)
    parts = []
    for side in range(2):
        parts.append(
            jnp.concatenate(
                [
                    forces[side, pl.ds(16 * UNROLL + k, count, stride=8), :]
                    for k in range(3)
                ],
                axis=1,
            )
        )
    high, low = high_low(jnp.concatenate(parts, axis=0))
    ids = jnp.concatenate([pair_rows[pl.ds(0, 1), :], pair_rows[pl.ds(1, 1), :]], axis=1)
    slots = lax.broadcasted_iota(jnp.int32, (devices, 2 * count), 0) * CAP
    for slot in range(CAP):
        chosen = jnp.where(slots + slot == ids, 1.0, 0.0).astype(BF16)
        value = jnp.dot(chosen, high, preferred_element_type=F32) + jnp.dot(
            chosen, low, preferred_element_type=F32
        )
        for k in range(3):
            out_ref[pl.ds(CAP * k + slot, devices, stride=ROWS), :] = value[
                :, k * WIDTH : (k + 1) * WIDTH
            ]

    def send_back(step, carry):
        bulk(step, out_ref, back_ref, ROWS, 0, BACK, 4).start()
        return carry

    lax.fori_loop(1, devices, send_back, 0)
    rows = pl.ds(pl.multiple_of(me * ROWS, ROWS), ROWS)
    back_ref[rows, :] = out_ref[rows, :]
    all_of(send_ref, got_ref, half, 0).wait_send()
    all_of(send_ref, got_ref, half, 2).wait_send()
    done = all_of(out_ref, back_ref, BACK, 4)
    done.wait_send()
    done.wait_recv()

    back = jnp.concatenate(
        [
            jnp.concatenate(
                [back_ref[pl.ds(CAP * k + slot, devices, stride=ROWS), :] for k in range(3)], axis=1
            )
            for slot in range(CAP)
        ],
        axis=0,
    )
    high, low = high_low(back)
    ids = jnp.concatenate([id_rows[pl.ds(slot, 1), :] for slot in range(CAP)], axis=1)
    for step in range(blocks // WIDTH):
        index = lax.broadcasted_iota(jnp.int32, (WIDTH, devices * CAP), 0) + step * WIDTH
        chosen = jnp.where(index == ids, 1.0, 0.0).astype(BF16)
        rows = pl.ds(step * WIDTH, WIDTH)
        o_ref[rows, :] = (
            o_ref[rows, :]
            + jnp.dot(chosen, high, preferred_element_type=F32)
            + jnp.dot(chosen, low, preferred_element_type=F32)
        )


def far_group(step, left, pos_ref, base_ref, o_ref, tile):
    for part in range(4):
        at = (step * 8 + part * 2) * ROWS
        both = jnp.concatenate(
            [base_ref[pl.ds(pl.multiple_of(at + i * ROWS, ROWS), ROWS), :] for i in range(2)], axis=1
        )
        high, low = high_low(both)
        forms = jnp.dot(
            left, jnp.concatenate([high, low, high], axis=0), preferred_element_type=F32
        )
        root = lax.rsqrt(forms[KC:])
        weight = forms[:KC] * root * (root * root)
        w = [weight[8 * v : 8 * v + 8] for v in range(8)]
        s = [w[2 * i] + w[2 * i + 1] for i in range(4)]
        sums = [
            1.5 * (s[3] - s[0]) + 0.5 * (s[2] - s[1]),
            (w[1] + w[3]) + (w[5] + w[7]),
            (s[0] + s[1]) + (s[2] + s[3]),
        ]
        for q, value in enumerate(sums):
            for i in range(2):
                tile[pl.ds(q * 64 + (part * 2 + i) * 8, 8), :] = value[:, i * WIDTH : (i + 1) * WIDTH]
    along_x, upper, t = (
        [tile[pl.ds(q * 64 + r, 8, stride=8), :] for r in range(8)] for q in range(3)
    )
    first = (t[0] + t[1]) + (t[2] + t[3])
    second = (t[4] + t[5]) + (t[6] + t[7])
    whole = first + second
    m = [t[i] + t[i + 4] for i in range(4)]
    centers = [
        sum(along_x[1:], along_x[0]),
        2.0 * sum(upper[1:], upper[0]) - 1.5 * first - 0.5 * second,
        1.5 * (m[3] - m[0]) + 0.5 * (m[2] - m[1]),
    ]
    rows = pl.ds(pl.multiple_of(step * 8, 8), 8)
    for k in range(3):
        column = pl.ds(k * WIDTH, WIDTH)
        o_ref[rows, column] = (pos_ref[rows, column] - MIDDLE) * whole - centers[k]


VM = pl.BlockSpec(memory_space=pltpu.VMEM)
SM = pl.BlockSpec(memory_space=pltpu.SMEM)
ANY = pl.BlockSpec(memory_space=pl.ANY)


def on_device(positions, vectors, send_slots, pairs, coarse):
    size_gx, size_yz = lax.axis_size("gx"), lax.axis_size("yz")
    devices = size_gx * size_yz
    blocks, slots, count = positions.shape[0], devices * CAP, pairs.shape[0]
    ids, pair_ids = send_slots[0].T, pairs.T

    def rows(number, width=WIDTH):
        return pltpu.VMEM((number, width), F32)

    dma = pltpu.SemaphoreType.DMA
    return pl.pallas_call(
        whole_kernel,
        name="forces",
        out_shape=jax.ShapeDtypeStruct((blocks, 3 * WIDTH), F32),
        in_specs=[SM, SM, VM, VM, VM, ANY, ANY],
        out_specs=VM,
        scratch_shapes=[
            rows(blocks, 3 * WIDTH),
            rows(blocks, 6 * WIDTH),
            pltpu.VMEM((blocks, 8, WIDTH), F32),
            rows(slots * 8),
            rows(slots * 8),
            rows(blocks * ROWS),
            rows(blocks, 9 * WIDTH),
            pltpu.VMEM((slots, 8, WIDTH), F32),
            pltpu.VMEM((slots, ROWS, WIDTH), F32),
            rows(count * WIDTH // 2, 2 * WIDTH),
            pltpu.VMEM((2, (count + 6 * UNROLL) * 8, WIDTH), F32),
            rows(devices * ROWS),
            rows(devices * ROWS),
            rows(8),
            pltpu.VMEM((size_yz, 8, WIDTH), F32),
            rows(8),
            pltpu.VMEM((size_gx, 8, WIDTH), F32),
            dma((2, LOADS)),
            dma((size_yz + size_gx,)),
            dma((size_yz + size_gx,)),
            dma((6,)),
            pltpu.SemaphoreType.REGULAR,
        ]
        + [rows(192)] * FAR_GROUPS
        + [pltpu.VMEM((2 * WIDTH, 2 * WIDTH), BF16)] * (2 * UNROLL),
        compiler_params=pltpu.CompilerParams(
            vmem_limit_bytes=VMEM_LIMIT, collective_id=0, has_side_effects=True
        ),
    )(ids, pair_ids, ids, pair_ids, coarse.reshape(1, blocks), positions, vectors)


def solution(mesh):
    placed = (
        P(("gx", "yz"), None),
        P(("gx", "yz"), None),
        P(("gx", "yz"), None, None),
        P(("gx", "yz"), None),
        P(("gx", "yz")),
    )
    return jax.shard_map(
        on_device, mesh=mesh, in_specs=placed, out_specs=P(("gx", "yz"), None), check_vma=False
    )
```

```python
import math

import jax
import jax.numpy as jnp
from jax import lax
from jax.experimental import pallas as pl
from jax.experimental.pallas import tpu as pltpu
from jax.sharding import PartitionSpec as P

MESH = pl.DeviceIdType.MESH
F32 = jnp.float32
BF16 = jnp.bfloat16
KC = 64
WIDTH = 128
MIDDLE = 2.0
ROWS = 16
UNROLL = 6
CUBE_UNROLL = 8
CAP = 4
BACK = 12
FAR_GROUPS = 4
SIDE_X = 4
LOADS = 8
VMEM_LIMIT = 54 * 2**20


def high_low(value):
    high = value.astype(BF16)
    return high, (value - high.astype(F32)).astype(BF16)


def couplings(tensor):
    scale = WIDTH**-0.25
    rows = [scale * math.sqrt(1.5) * tensor[k][k] for k in range(3)]
    for k, l in ((0, 1), (0, 2), (1, 2)):
        rows.append(scale * math.sqrt(0.75) * (tensor[k][l] + tensor[l][k]))
        rows.append(scale * 0.5 * (tensor[k][l] - tensor[l][k]))
    return rows


def features(place, tensor):
    square = place[0] * place[0] + place[1] * place[1] + place[2] * place[2] + 0.125
    upper = square.astype(BF16).astype(F32)
    one = jnp.ones_like(square)
    return couplings(tensor) + list(place) + [upper, square - upper, one, one]


def pack_group(step, pos_ref, vec_ref, base_ref, table, packed):
    rows = pl.ds(pl.multiple_of(step * 8, 8), 8)
    place = [pos_ref[rows, pl.ds(k * WIDTH, WIDTH)] - MIDDLE for k in range(3)]
    line = [vec_ref[rows, pl.ds(k * WIDTH, WIDTH)] for k in range(3)]
    burg = [vec_ref[rows, pl.ds((3 + k) * WIDTH, WIDTH)] for k in range(3)]
    for row, value in enumerate(features(place, [[b * l for l in line] for b in burg])):
        base_ref[pl.ds(step * 8 * ROWS + row, 8, stride=ROWS), :] = value
        if row < 9:
            table[rows, pl.ds(row * WIDTH, WIDTH)] = value
    square = line[0] * line[0] + line[1] * line[1] + line[2] * line[2]
    inverse = lax.rsqrt(jnp.maximum(square, 1e-36))
    side = jnp.where(line[2] < 0, -inverse, inverse)
    length = square * side
    tilt = 1.0 / (1.0 + line[2] * side)
    out = place + [b * length for b in burg] + [line[0] * side * tilt, line[1] * side * tilt]
    for row, value in enumerate(out):
        packed[pl.ds(step * 64 + row, 8, stride=8), :] = value


def cell_sums(coarse_ref, table):
    blocks = table.shape[0]
    cells = lax.broadcasted_iota(jnp.int32, (KC, blocks), 0)
    chosen = jnp.where(cells == coarse_ref[...], 1.0, 0.0).astype(BF16)
    parts = []
    for m in range(9):
        high, low = high_low(table[:, m * WIDTH : (m + 1) * WIDTH])
        parts.append(
            jnp.dot(chosen, high, preferred_element_type=F32)
            + jnp.dot(chosen, low, preferred_element_type=F32)
        )
    high, low = high_low(jnp.concatenate(parts, axis=1))
    row = lax.broadcasted_iota(jnp.int32, (ROWS, 9 * WIDTH), 0)
    lane = lax.broadcasted_iota(jnp.int32, (ROWS, 9 * WIDTH), 1)
    along = jnp.where((lane >= row * WIDTH) & (lane < row * WIDTH + WIDTH), 1.0, 0.0).astype(BF16)
    sums = [
        lax.dot_general(along, value, (((1,), (1,)), ((), ())), preferred_element_type=F32)
        for value in (high, low)
    ]
    sums = sums[0] + sums[1]
    return jnp.concatenate([sums[:8], sums[8:]], axis=1)


def far_left(sums, norm):
    row = lax.broadcasted_iota(jnp.int32, (ROWS, KC), 0)
    cell = lax.broadcasted_iota(jnp.int32, (ROWS, KC), 1)
    turned = (row == 4) | (row == 6) | (row == 8)
    square = WIDTH**-0.5
    strength = sums * jnp.where(turned, 2.0 / square * norm, norm / (1.5 * square))
    centers = [(c + (0.5 - MIDDLE)).astype(F32) for c in (cell // 16, cell // 4 % 4, cell % 4)]
    whole = centers[0] * centers[0] + centers[1] * centers[1] + centers[2] * centers[2]
    squares = jnp.where((row == 12) | (row == 13), 1.0, 0.0)
    squares = jnp.where(row == 14, whole + (1.0 - 0.125), squares)
    for k in range(3):
        squares = jnp.where(row == 9 + k, -2.0 * centers[k], squares)
    left = jnp.transpose(jnp.concatenate([strength, squares], axis=1))
    high, low = high_low(left)
    return jnp.concatenate([high, high, low], axis=1)


def stacked(tile):
    return jnp.concatenate(high_low(tile), axis=0)


def beside(first, second):
    blank = jnp.zeros_like(first)
    return jnp.concatenate(
        [jnp.concatenate([first, blank], axis=1), jnp.concatenate([blank, second], axis=1)], axis=0
    )


def forms_of(lefts, rights):
    return lax.dot_general(
        jnp.concatenate(lefts, axis=0),
        beside(*rights),
        (((0,), (0,)), ((), ())),
        preferred_element_type=F32,
    )


def whole_kernel(
    ids_hbm,
    pairs_hbm,
    coarse_hbm,
    pos_hbm,
    vec_hbm,
    o_ref,
    ids_ref,
    pairs_ref,
    id_rows,
    pair_rows,
    coarse_ref,
    pos_ref,
    vec_ref,
    packed,
    send_ref,
    got_ref,
    base_ref,
    table,
    place_base,
    form_base,
    cubes,
    forces,
    out_ref,
    back_ref,
    mine,
    near,
    total,
    far,
    load_sem,
    send_sem,
    recv_sem,
    bulk_sem,
    small_sem,
    round_sem,
    *buffers,
):
    packed_rows, place_rows_ref, form_rows_ref = [
        ref.reshape(ref.shape[0] * ref.shape[1], WIDTH) for ref in (packed, place_base, form_base)
    ]
    tiles, matrices = buffers[:FAR_GROUPS], buffers[FAR_GROUPS:]
    gx, yz = lax.axis_index("gx"), lax.axis_index("yz")
    size_gx, size_yz = lax.axis_size("gx"), lax.axis_size("yz")
    devices = size_gx * size_yz
    me = gx * size_yz + yz
    blocks = pos_ref.shape[0]
    count = pairs_ref.shape[1]
    loaded = blocks // LOADS

    def along_yz(step):
        return gx, lax.rem(yz + step, size_yz)

    def along_gx(step):
        return lax.rem(gx + step, size_gx), yz

    def loads(step):
        rows = pl.ds(pl.multiple_of(step * loaded, loaded), loaded)
        return [
            pltpu.make_async_copy(source.at[rows], target.at[rows], load_sem.at[k, step])
            for k, (source, target) in enumerate(((pos_hbm, pos_ref), (vec_hbm, vec_ref)))
        ]

    barrier = pltpu.get_barrier_semaphore()
    for turn, size in ((along_yz, size_yz), (along_gx, size_gx)):
        for step in range(1, size):
            pl.semaphore_signal(barrier, inc=1, device_id=turn(step), device_id_type=MESH)
    small = [
        pltpu.make_async_copy(source, target, small_sem.at[k])
        for k, (source, target) in enumerate(
            (
                (ids_hbm, ids_ref),
                (coarse_hbm, coarse_ref),
                (pairs_hbm, pairs_ref),
                (ids_hbm, id_rows),
                (pairs_hbm, pair_rows),
            )
        )
    ]
    for step in range(LOADS):
        for copy in loads(step):
            copy.start()
    for copy in small:
        copy.start()

    def pack(step, carry):
        for copy in loads(step):
            copy.wait()

        def group(inner, carry):
            pack_group(step * (loaded // 8) + inner, pos_ref, vec_ref, base_ref, table, packed_rows)
            return carry

        return lax.fori_loop(0, loaded // 8, group, carry)

    lax.fori_loop(0, LOADS, pack, 0)
    pl.semaphore_wait(barrier, size_yz + size_gx - 2)
    for step in range(1, size_yz):
        pl.semaphore_signal(round_sem, inc=1, device_id=along_yz(step), device_id_type=MESH)
    for copy in small:
        copy.wait()

    def exchange(source, held, turn, size, sem):
        return [
            pltpu.make_async_remote_copy(
                src_ref=source,
                dst_ref=held.at[step],
                send_sem=send_sem.at[sem + step],
                recv_sem=recv_sem.at[sem + step],
                device_id=turn(step),
                device_id_type=MESH,
            )
            for step in range(1, size)
        ]

    def gathered(source, held, copies):
        for copy in copies:
            copy.wait()
        result = source[...]
        for step in range(1, len(copies) + 1):
            result = result + held[step]
        return result

    chunk = CAP * 8
    half = chunk // 2

    def pick(device):
        for slot in range(CAP):
            source = jnp.maximum(ids_ref[slot, device], 0)
            send_ref[pl.ds(device * chunk + slot, 8, stride=CAP), :] = packed[
                source
            ]

    def bulk(to, source, target, pitch, at, size, sem):
        to_gx, to_yz = to
        device = to_gx * size_yz + to_yz
        return pltpu.make_async_remote_copy(
            src_ref=source.at[pl.ds(pl.multiple_of(device * pitch + at, 8), size)],
            dst_ref=target.at[pl.ds(pl.multiple_of(me * pitch + at, 8), size)],
            send_sem=bulk_sem.at[sem],
            recv_sem=bulk_sem.at[sem + 1],
            device_id=(to_gx, to_yz),
            device_id_type=MESH,
        )

    def all_of(source, target, size, sem):
        rows = pl.ds(0, (devices - 1) * size)
        return pltpu.make_async_remote_copy(
            src_ref=source.at[rows],
            dst_ref=target.at[rows],
            send_sem=bulk_sem.at[sem],
            recv_sem=bulk_sem.at[sem + 1],
            device_id=along_yz(1),
            device_id_type=MESH,
        )

    def to_axes(send):
        def one(turn):
            def step(number, carry):
                send(turn(number))
                return carry

            return step

        lax.fori_loop(1, size_yz, one(along_yz), 0)
        lax.fori_loop(1, size_gx, one(along_gx), 0)

    def aside(send, step):
        for part in range(size_yz - 1):
            turned = lax.rem(step + part, size_yz - 1)
            send((lax.rem(gx + step, size_gx), lax.rem(yz + 1 + turned, size_yz)))

    def to_rest(send):
        def one(step, carry):
            aside(send, step)
            return carry

        lax.fori_loop(1, size_gx, one, 0)

    side_x, side_z = SIDE_X, size_yz // 2
    side_y = size_gx // side_x
    here = (gx // side_x, lax.rem(gx, side_x), yz // 2, lax.rem(yz, 2))

    def to_chips(send):
        def turn(second, third, core, first):
            for ahead in range(first, side_y):
                y = lax.rem(here[0] + ahead, side_y)
                x = lax.rem(here[1] + ahead + second, side_x)
                z = lax.rem(here[2] + ahead + second + third, side_z)
                send((y * side_x + x, z * 2 + lax.rem(here[3] + core, 2)))

        def one(step, carry):
            turn(
                lax.rem(step, side_x),
                lax.rem(step // side_x, side_z),
                step // (side_x * side_z),
                0,
            )
            return carry

        turn(0, 0, 0, 1)
        lax.fori_loop(1, 2 * side_x * side_z, one, 0)

    def send_first(to):
        pick(to[0] * size_yz + to[1])
        bulk(to, send_ref, got_ref, chunk, 0, half, 0).start()

    def send_second(to):
        bulk(to, send_ref, got_ref, chunk, half, half, 2).start()

    def send_back(to):
        bulk(to, out_ref, back_ref, ROWS, 0, BACK, 4).start()

    to_axes(send_first)
    mine[...] = cell_sums(coarse_ref, table)
    over_yz = exchange(mine, near, along_yz, size_yz, 0)
    over_gx = exchange(total, far, along_gx, size_gx, size_yz)
    for copy in over_yz:
        copy.start()
    pl.semaphore_wait(round_sem, size_yz - 1)
    to_rest(send_first)
    to_axes(send_second)
    to_rest(send_second)
    total[...] = gathered(mine, near, over_yz)
    for copy in over_gx:
        copy.start()
    pick(me)
    rows = pl.ds(pl.multiple_of(me * chunk, chunk), chunk)
    got_ref[rows, :] = send_ref[rows, :]
    for matrix in matrices:
        matrix[...] = jnp.zeros_like(matrix)
    form_base[...] = jnp.zeros_like(form_base)

    def came(step, slot, first, last):
        return [
            got_ref[pl.ds(step * 8 * chunk + CAP * k + slot, 8, stride=chunk), :]
            for k in range(first, last)
        ]

    all_of(send_ref, got_ref, half, 0).wait_recv()

    def place_rows(step, carry):
        for slot in range(CAP):
            place = came(step, slot, 0, 3)
            square = place[0] * place[0] + place[1] * place[1] + place[2] * place[2] + 0.125
            upper = square.astype(BF16).astype(F32)
            one = jnp.ones_like(square)
            values = place + [upper, square - upper, one, one, jnp.zeros_like(square)]
            for row, value in enumerate(values):
                place_rows_ref[pl.ds(step * 64 * CAP + slot * 8 + row, 8, stride=8 * CAP), :] = value
        return carry

    lax.fori_loop(0, devices // 8, place_rows, 0)
    row = lax.broadcasted_iota(jnp.int32, (8, WIDTH), 0)

    def tile_of(base, side, number):
        return base[jnp.maximum(pairs_ref[side, number], 0)]

    def cube_step(step, carry):
        for part in range(CUBE_UNROLL):
            number = (step * CUBE_UNROLL + part) * 2
            lefts, rights = [], []
            for i in range(2):
                value = stacked(tile_of(place_base, 0, number + i))
                lefts += [value, value]
                last = tile_of(place_base, 1, number + i)
                turned = pltpu.roll(last, 2, 0)
                last = jnp.where(
                    row < 3, -2.0 * last, jnp.where(row < 5, 1.0, jnp.where(row < 7, turned, 0.0))
                )
                high, low = high_low(last)
                rights.append(jnp.concatenate([high, high, low, low], axis=0))
            root = lax.rsqrt(forms_of(lefts, rights))
            rows = pl.ds(pl.multiple_of(number * (WIDTH // 2), WIDTH), WIDTH)
            cubes[rows, :] = root * (root * root)
        return carry

    lax.fori_loop(0, count // (2 * CUBE_UNROLL), cube_step, 0)
    all_of(send_ref, got_ref, half, 2).wait_recv()

    def form_rows(step, carry):
        for slot in range(CAP):
            got = came(step, slot, 3, 8)
            square = got[3] * got[3] + got[4] * got[4]
            inverse = 1.0 / (1.0 + square)
            line = [2.0 * got[3] * inverse, 2.0 * got[4] * inverse, (1.0 - square) * inverse]
            for row, value in enumerate(couplings([[b * l for l in line] for b in got[:3]])):
                form_rows_ref[
                    pl.ds(step * 8 * ROWS * CAP + slot * ROWS + row, 8, stride=ROWS * CAP), :
                ] = value
        return carry

    lax.fori_loop(0, devices // 8, form_rows, 0)

    def fill(number, matrix):
        lefts, rights = [], []
        for i in range(2):
            high, low = high_low(tile_of(form_base, 0, number + i))
            lefts += [high, high, low]
            high, low = high_low(tile_of(form_base, 1, number + i))
            rights.append(jnp.concatenate([high, low, high], axis=0))
        rows = pl.ds(pl.multiple_of(number * (WIDTH // 2), WIDTH), WIDTH)
        high, low = high_low(forms_of(lefts, rights) * cubes[rows, :])
        matrix[pl.ds(0, WIDTH), :] = high
        matrix[pl.ds(WIDTH, WIDTH), :] = low

    def drain(number, at, matrix):
        value = matrix[...]
        places = [[tile_of(place_base, side, number + i) for i in range(2)] for side in range(2)]
        first, second = [[stacked(tile) for tile in side] for side in places]
        on_b = jnp.dot(
            jnp.concatenate([jnp.concatenate([p, p], axis=1) for p in first], axis=0),
            value,
            preferred_element_type=F32,
        )
        on_a = lax.dot_general(
            beside(*second), value, (((1,), (1,)), ((), ())), preferred_element_type=F32
        )
        for i in range(2):
            on_first = on_a[i * ROWS : (i + 1) * ROWS]
            on_first = on_first[:, :WIDTH] + on_first[:, WIDTH:]
            on_second = on_b[i * ROWS : (i + 1) * ROWS, i * WIDTH : (i + 1) * WIDTH]
            for side, got in enumerate((on_first, on_second)):
                force = places[side][i] * got[5:6] - (got[:8] + got[8:])
                forces[side, pl.ds(pl.multiple_of((at + i) * 8, 8), 8), :] = force

    even, odd = matrices[:UNROLL], matrices[UNROLL:]

    def half_step(number, filled, drained):
        for part in range(UNROLL):
            fill(jnp.minimum(number + 2 * part, count - 2), filled[part])
            at = number + 2 * part
            before = jnp.clip(at - 2 * UNROLL, 0, count - 2)
            drain(before, at, drained[part])

    def pair_step(step, carry):
        half_step(step * 4 * UNROLL, even, odd)
        half_step(step * 4 * UNROLL + 2 * UNROLL, odd, even)
        return carry

    lax.fori_loop(0, pl.cdiv(count + 2 * UNROLL, 4 * UNROLL), pair_step, 0)
    parts = []
    for side in range(2):
        parts.append(
            jnp.concatenate(
                [
                    forces[side, pl.ds(16 * UNROLL + k, count, stride=8), :]
                    for k in range(3)
                ],
                axis=1,
            )
        )
    high, low = high_low(jnp.concatenate(parts, axis=0))
    ids = jnp.concatenate([pair_rows[pl.ds(0, 1), :], pair_rows[pl.ds(1, 1), :]], axis=1)
    slots = lax.broadcasted_iota(jnp.int32, (devices, 2 * count), 0) * CAP
    for slot in range(CAP):
        chosen = jnp.where(slots + slot == ids, 1.0, 0.0).astype(BF16)
        value = jnp.dot(chosen, high, preferred_element_type=F32) + jnp.dot(
            chosen, low, preferred_element_type=F32
        )
        for k in range(3):
            out_ref[pl.ds(CAP * k + slot, devices, stride=ROWS), :] = value[
                :, k * WIDTH : (k + 1) * WIDTH
            ]

    to_chips(send_back)
    sums = gathered(total, far, over_gx)
    left = far_left(
        jnp.concatenate([sums[:, :KC], sums[:, KC:]], axis=0),
        1.0 / (math.sqrt(blocks * devices * WIDTH / KC) * math.sqrt(KC)),
    )

    def far_step(step, carry):
        for part in range(FAR_GROUPS):
            far_group(step * FAR_GROUPS + part, left, pos_ref, base_ref, o_ref, tiles[part])
        return carry

    lax.fori_loop(0, blocks // (8 * FAR_GROUPS), far_step, 0)
    rows = pl.ds(pl.multiple_of(me * ROWS, ROWS), ROWS)
    back_ref[rows, :] = out_ref[rows, :]
    all_of(send_ref, got_ref, half, 0).wait_send()
    all_of(send_ref, got_ref, half, 2).wait_send()
    done = all_of(out_ref, back_ref, BACK, 4)
    done.wait_send()
    done.wait_recv()

    back = jnp.concatenate(
        [
            jnp.concatenate(
                [back_ref[pl.ds(CAP * k + slot, devices, stride=ROWS), :] for k in range(3)], axis=1
            )
            for slot in range(CAP)
        ],
        axis=0,
    )
    high, low = high_low(back)
    ids = jnp.concatenate([id_rows[pl.ds(slot, 1), :] for slot in range(CAP)], axis=1)
    for step in range(blocks // WIDTH):
        index = lax.broadcasted_iota(jnp.int32, (WIDTH, devices * CAP), 0) + step * WIDTH
        chosen = jnp.where(index == ids, 1.0, 0.0).astype(BF16)
        rows = pl.ds(step * WIDTH, WIDTH)
        o_ref[rows, :] = (
            o_ref[rows, :]
            + jnp.dot(chosen, high, preferred_element_type=F32)
            + jnp.dot(chosen, low, preferred_element_type=F32)
        )


def far_group(step, left, pos_ref, base_ref, o_ref, tile):
    for part in range(4):
        at = (step * 8 + part * 2) * ROWS
        both = jnp.concatenate(
            [base_ref[pl.ds(pl.multiple_of(at + i * ROWS, ROWS), ROWS), :] for i in range(2)], axis=1
        )
        high, low = high_low(both)
        forms = jnp.dot(
            left, jnp.concatenate([high, low, high], axis=0), preferred_element_type=F32
        )
        root = lax.rsqrt(forms[KC:])
        weight = forms[:KC] * root * (root * root)
        w = [weight[8 * v : 8 * v + 8] for v in range(8)]
        s = [w[2 * i] + w[2 * i + 1] for i in range(4)]
        sums = [
            1.5 * (s[3] - s[0]) + 0.5 * (s[2] - s[1]),
            (w[1] + w[3]) + (w[5] + w[7]),
            (s[0] + s[1]) + (s[2] + s[3]),
        ]
        for q, value in enumerate(sums):
            for i in range(2):
                tile[pl.ds(q * 64 + (part * 2 + i) * 8, 8), :] = value[:, i * WIDTH : (i + 1) * WIDTH]
    along_x, upper, t = (
        [tile[pl.ds(q * 64 + r, 8, stride=8), :] for r in range(8)] for q in range(3)
    )
    first = (t[0] + t[1]) + (t[2] + t[3])
    second = (t[4] + t[5]) + (t[6] + t[7])
    whole = first + second
    m = [t[i] + t[i + 4] for i in range(4)]
    centers = [
        sum(along_x[1:], along_x[0]),
        2.0 * sum(upper[1:], upper[0]) - 1.5 * first - 0.5 * second,
        1.5 * (m[3] - m[0]) + 0.5 * (m[2] - m[1]),
    ]
    rows = pl.ds(pl.multiple_of(step * 8, 8), 8)
    for k in range(3):
        column = pl.ds(k * WIDTH, WIDTH)
        o_ref[rows, column] = (pos_ref[rows, column] - MIDDLE) * whole - centers[k]


VM = pl.BlockSpec(memory_space=pltpu.VMEM)


def on_device(positions, vectors, send_slots, pairs, coarse):
    size_gx, size_yz = lax.axis_size("gx"), lax.axis_size("yz")
    devices = size_gx * size_yz
    blocks, slots, count = positions.shape[0], devices * CAP, pairs.shape[0]
    ids, pair_ids = send_slots[0].T, pairs.T

    def rows(number, width=WIDTH):
        return pltpu.VMEM((number, width), F32)

    dma = pltpu.SemaphoreType.DMA
    return pl.pallas_call(
        whole_kernel,
        name="forces",
        out_shape=jax.ShapeDtypeStruct((blocks, 3 * WIDTH), F32),
        in_specs=[pl.BlockSpec(memory_space=pltpu.HBM)] * 5,
        out_specs=VM,
        scratch_shapes=[
            pltpu.SMEM((CAP, devices), jnp.int32),
            pltpu.SMEM((2, count), jnp.int32),
            pltpu.VMEM((CAP, devices), jnp.int32),
            pltpu.VMEM((2, count), jnp.int32),
            pltpu.VMEM((1, blocks), jnp.int32),
            rows(blocks, 3 * WIDTH),
            rows(blocks, 6 * WIDTH),
            pltpu.VMEM((blocks, 8, WIDTH), F32),
            rows(slots * 8),
            rows(slots * 8),
            rows(blocks * ROWS),
            rows(blocks, 9 * WIDTH),
            pltpu.VMEM((slots, 8, WIDTH), F32),
            pltpu.VMEM((slots, ROWS, WIDTH), F32),
            rows(count * WIDTH // 2, 2 * WIDTH),
            pltpu.VMEM((2, (count + 6 * UNROLL) * 8, WIDTH), F32),
            rows(devices * ROWS),
            rows(devices * ROWS),
            rows(8),
            pltpu.VMEM((size_yz, 8, WIDTH), F32),
            rows(8),
            pltpu.VMEM((size_gx, 8, WIDTH), F32),
            dma((2, LOADS)),
            dma((size_yz + size_gx,)),
            dma((size_yz + size_gx,)),
            dma((6,)),
            dma((5,)),
            pltpu.SemaphoreType.REGULAR,
        ]
        + [rows(192)] * FAR_GROUPS
        + [pltpu.VMEM((2 * WIDTH, 2 * WIDTH), BF16)] * (2 * UNROLL),
        compiler_params=pltpu.CompilerParams(
            vmem_limit_bytes=VMEM_LIMIT, collective_id=0, has_side_effects=True
        ),
    )(ids, pair_ids, coarse.reshape(1, blocks), positions, vectors)


def solution(mesh):
    placed = (
        P(("gx", "yz"), None),
        P(("gx", "yz"), None),
        P(("gx", "yz"), None, None),
        P(("gx", "yz"), None),
        P(("gx", "yz")),
    )
    return jax.shard_map(
        on_device, mesh=mesh, in_specs=placed, out_specs=P(("gx", "yz"), None), check_vma=False
    )
```

```python
import math

import jax
import jax.numpy as jnp
from jax import lax
from jax.experimental import pallas as pl
from jax.experimental.pallas import tpu as pltpu
from jax.sharding import PartitionSpec as P

MESH = pl.DeviceIdType.MESH
F32 = jnp.float32
BF16 = jnp.bfloat16
KC = 64
WIDTH = 128
MIDDLE = 2.0
ROWS = 16
UNROLL = 8
CUBE_UNROLL = 8
CAP = 4
BACK = 12
FAR_GROUPS = 4
SIDE_X = 4
LOADS = 8
VMEM_LIMIT = 54 * 2**20


def high_low(value):
    high = value.astype(BF16)
    return high, (value - high.astype(F32)).astype(BF16)


def couplings(tensor):
    scale = WIDTH**-0.25
    rows = [scale * math.sqrt(1.5) * tensor[k][k] for k in range(3)]
    for k, l in ((0, 1), (0, 2), (1, 2)):
        rows.append(scale * math.sqrt(0.75) * (tensor[k][l] + tensor[l][k]))
        rows.append(scale * 0.5 * (tensor[k][l] - tensor[l][k]))
    return rows


def features(place, tensor):
    square = place[0] * place[0] + place[1] * place[1] + place[2] * place[2] + 0.125
    upper = square.astype(BF16).astype(F32)
    one = jnp.ones_like(square)
    return couplings(tensor) + list(place) + [upper, square - upper, one, one]


def pack_group(step, pos_ref, vec_ref, base_ref, table, packed):
    rows = pl.ds(pl.multiple_of(step * 8, 8), 8)
    place = [pos_ref[rows, pl.ds(k * WIDTH, WIDTH)] - MIDDLE for k in range(3)]
    line = [vec_ref[rows, pl.ds(k * WIDTH, WIDTH)] for k in range(3)]
    burg = [vec_ref[rows, pl.ds((3 + k) * WIDTH, WIDTH)] for k in range(3)]
    for row, value in enumerate(features(place, [[b * l for l in line] for b in burg])):
        base_ref[pl.ds(step * 8 * ROWS + row, 8, stride=ROWS), :] = value
        if row < 9:
            table[rows, pl.ds(row * WIDTH, WIDTH)] = value
    square = line[0] * line[0] + line[1] * line[1] + line[2] * line[2]
    inverse = lax.rsqrt(jnp.maximum(square, 1e-36))
    side = jnp.where(line[2] < 0, -inverse, inverse)
    length = square * side
    tilt = 1.0 / (1.0 + line[2] * side)
    out = place + [b * length for b in burg] + [line[0] * side * tilt, line[1] * side * tilt]
    for row, value in enumerate(out):
        packed[pl.ds(step * 64 + row, 8, stride=8), :] = value


def cell_sums(coarse_ref, table):
    blocks = table.shape[0]
    cells = lax.broadcasted_iota(jnp.int32, (KC, blocks), 0)
    chosen = jnp.where(cells == coarse_ref[...], 1.0, 0.0).astype(BF16)
    parts = []
    for m in range(9):
        high, low = high_low(table[:, m * WIDTH : (m + 1) * WIDTH])
        parts.append(
            jnp.dot(chosen, high, preferred_element_type=F32)
            + jnp.dot(chosen, low, preferred_element_type=F32)
        )
    high, low = high_low(jnp.concatenate(parts, axis=1))
    row = lax.broadcasted_iota(jnp.int32, (ROWS, 9 * WIDTH), 0)
    lane = lax.broadcasted_iota(jnp.int32, (ROWS, 9 * WIDTH), 1)
    along = jnp.where((lane >= row * WIDTH) & (lane < row * WIDTH + WIDTH), 1.0, 0.0).astype(BF16)
    sums = [
        lax.dot_general(along, value, (((1,), (1,)), ((), ())), preferred_element_type=F32)
        for value in (high, low)
    ]
    sums = sums[0] + sums[1]
    return jnp.concatenate([sums[:8], sums[8:]], axis=1)


def far_left(sums, norm):
    row = lax.broadcasted_iota(jnp.int32, (ROWS, KC), 0)
    cell = lax.broadcasted_iota(jnp.int32, (ROWS, KC), 1)
    turned = (row == 4) | (row == 6) | (row == 8)
    square = WIDTH**-0.5
    strength = sums * jnp.where(turned, 2.0 / square * norm, norm / (1.5 * square))
    centers = [(c + (0.5 - MIDDLE)).astype(F32) for c in (cell // 16, cell // 4 % 4, cell % 4)]
    whole = centers[0] * centers[0] + centers[1] * centers[1] + centers[2] * centers[2]
    squares = jnp.where((row == 12) | (row == 13), 1.0, 0.0)
    squares = jnp.where(row == 14, whole + (1.0 - 0.125), squares)
    for k in range(3):
        squares = jnp.where(row == 9 + k, -2.0 * centers[k], squares)
    left = jnp.transpose(jnp.concatenate([strength, squares], axis=1))
    high, low = high_low(left)
    return jnp.concatenate([high, high, low], axis=1)


def stacked(tile):
    return jnp.concatenate(high_low(tile), axis=0)


def beside(first, second):
    blank = jnp.zeros_like(first)
    return jnp.concatenate(
        [jnp.concatenate([first, blank], axis=1), jnp.concatenate([blank, second], axis=1)], axis=0
    )


def forms_of(lefts, rights):
    return lax.dot_general(
        jnp.concatenate(lefts, axis=0),
        beside(*rights),
        (((0,), (0,)), ((), ())),
        preferred_element_type=F32,
    )


def whole_kernel(
    ids_hbm,
    pairs_hbm,
    coarse_hbm,
    pos_hbm,
    vec_hbm,
    o_ref,
    ids_ref,
    pairs_ref,
    id_rows,
    pair_rows,
    coarse_ref,
    pos_ref,
    vec_ref,
    packed,
    send_ref,
    got_ref,
    base_ref,
    table,
    place_base,
    form_base,
    cubes,
    forces,
    out_ref,
    back_ref,
    mine,
    near,
    total,
    far,
    load_sem,
    send_sem,
    recv_sem,
    bulk_sem,
    small_sem,
    round_sem,
    *buffers,
):
    packed_rows, place_rows_ref, form_rows_ref = [
        ref.reshape(ref.shape[0] * ref.shape[1], WIDTH) for ref in (packed, place_base, form_base)
    ]
    tiles, matrices = buffers[:FAR_GROUPS], buffers[FAR_GROUPS:]
    gx, yz = lax.axis_index("gx"), lax.axis_index("yz")
    size_gx, size_yz = lax.axis_size("gx"), lax.axis_size("yz")
    devices = size_gx * size_yz
    me = gx * size_yz + yz
    blocks = pos_ref.shape[0]
    count = pairs_ref.shape[1]
    loaded = blocks // LOADS

    def along_yz(step):
        return gx, lax.rem(yz + step, size_yz)

    def along_gx(step):
        return lax.rem(gx + step, size_gx), yz

    def loads(step):
        rows = pl.ds(pl.multiple_of(step * loaded, loaded), loaded)
        return [
            pltpu.make_async_copy(source.at[rows], target.at[rows], load_sem.at[k, step])
            for k, (source, target) in enumerate(((pos_hbm, pos_ref), (vec_hbm, vec_ref)))
        ]

    barrier = pltpu.get_barrier_semaphore()
    for turn, size in ((along_yz, size_yz), (along_gx, size_gx)):
        for step in range(1, size):
            pl.semaphore_signal(barrier, inc=1, device_id=turn(step), device_id_type=MESH)
    small = [
        pltpu.make_async_copy(source, target, small_sem.at[k])
        for k, (source, target) in enumerate(
            (
                (ids_hbm, ids_ref),
                (coarse_hbm, coarse_ref),
                (pairs_hbm, pairs_ref),
                (ids_hbm, id_rows),
                (pairs_hbm, pair_rows),
            )
        )
    ]
    for step in range(LOADS):
        for copy in loads(step):
            copy.start()
    for copy in small:
        copy.start()

    def pack(step, carry):
        for copy in loads(step):
            copy.wait()

        def group(inner, carry):
            pack_group(step * (loaded // 8) + inner, pos_ref, vec_ref, base_ref, table, packed_rows)
            return carry

        return lax.fori_loop(0, loaded // 8, group, carry)

    lax.fori_loop(0, LOADS, pack, 0)
    pl.semaphore_wait(barrier, size_yz + size_gx - 2)
    for step in range(1, size_yz):
        pl.semaphore_signal(round_sem, inc=1, device_id=along_yz(step), device_id_type=MESH)
    for copy in small:
        copy.wait()

    def exchange(source, held, turn, size, sem):
        return [
            pltpu.make_async_remote_copy(
                src_ref=source,
                dst_ref=held.at[step],
                send_sem=send_sem.at[sem + step],
                recv_sem=recv_sem.at[sem + step],
                device_id=turn(step),
                device_id_type=MESH,
            )
            for step in range(1, size)
        ]

    def gathered(source, held, copies):
        for copy in copies:
            copy.wait()
        result = source[...]
        for step in range(1, len(copies) + 1):
            result = result + held[step]
        return result

    chunk = CAP * 8
    half = chunk // 2

    def pick(device):
        for slot in range(CAP):
            source = jnp.maximum(ids_ref[slot, device], 0)
            send_ref[pl.ds(device * chunk + slot, 8, stride=CAP), :] = packed[
                source
            ]

    def bulk(to, source, target, pitch, at, size, sem):
        to_gx, to_yz = to
        device = to_gx * size_yz + to_yz
        return pltpu.make_async_remote_copy(
            src_ref=source.at[pl.ds(pl.multiple_of(device * pitch + at, 8), size)],
            dst_ref=target.at[pl.ds(pl.multiple_of(me * pitch + at, 8), size)],
            send_sem=bulk_sem.at[sem],
            recv_sem=bulk_sem.at[sem + 1],
            device_id=(to_gx, to_yz),
            device_id_type=MESH,
        )

    def all_of(source, target, size, sem):
        rows = pl.ds(0, (devices - 1) * size)
        return pltpu.make_async_remote_copy(
            src_ref=source.at[rows],
            dst_ref=target.at[rows],
            send_sem=bulk_sem.at[sem],
            recv_sem=bulk_sem.at[sem + 1],
            device_id=along_yz(1),
            device_id_type=MESH,
        )

    def to_axes(send):
        def one(turn):
            def step(number, carry):
                send(turn(number))
                return carry

            return step

        lax.fori_loop(1, size_yz, one(along_yz), 0)
        lax.fori_loop(1, size_gx, one(along_gx), 0)

    def aside(send, step):
        for part in range(size_yz - 1):
            turned = lax.rem(step + part, size_yz - 1)
            send((lax.rem(gx + step, size_gx), lax.rem(yz + 1 + turned, size_yz)))

    def to_rest(send):
        def one(step, carry):
            aside(send, step)
            return carry

        lax.fori_loop(1, size_gx, one, 0)

    side_x, side_z = SIDE_X, size_yz // 2
    side_y = size_gx // side_x
    here = (gx // side_x, lax.rem(gx, side_x), yz // 2, lax.rem(yz, 2))

    def to_chips(send):
        def turn(second, third, core, first):
            for ahead in range(first, side_y):
                y = lax.rem(here[0] + ahead, side_y)
                x = lax.rem(here[1] + ahead + second, side_x)
                z = lax.rem(here[2] + ahead + second + third, side_z)
                send((y * side_x + x, z * 2 + lax.rem(here[3] + core, 2)))

        def one(step, carry):
            turn(
                lax.rem(step, side_x),
                lax.rem(step // side_x, side_z),
                step // (side_x * side_z),
                0,
            )
            return carry

        turn(0, 0, 0, 1)
        lax.fori_loop(1, 2 * side_x * side_z, one, 0)

    def send_first(to):
        pick(to[0] * size_yz + to[1])
        bulk(to, send_ref, got_ref, chunk, 0, half, 0).start()

    def send_second(to):
        bulk(to, send_ref, got_ref, chunk, half, half, 2).start()

    def send_back(to):
        bulk(to, out_ref, back_ref, ROWS, 0, BACK, 4).start()

    to_axes(send_first)
    mine[...] = cell_sums(coarse_ref, table)
    over_yz = exchange(mine, near, along_yz, size_yz, 0)
    over_gx = exchange(total, far, along_gx, size_gx, size_yz)
    for copy in over_yz:
        copy.start()
    pl.semaphore_wait(round_sem, size_yz - 1)
    to_rest(send_first)
    to_axes(send_second)
    to_rest(send_second)
    total[...] = gathered(mine, near, over_yz)
    for copy in over_gx:
        copy.start()
    pick(me)
    rows = pl.ds(pl.multiple_of(me * chunk, chunk), chunk)
    got_ref[rows, :] = send_ref[rows, :]
    form_base[...] = jnp.zeros_like(form_base)

    def came(step, slot, first, last):
        return [
            got_ref[pl.ds(step * 8 * chunk + CAP * k + slot, 8, stride=chunk), :]
            for k in range(first, last)
        ]

    all_of(send_ref, got_ref, half, 0).wait_recv()

    def place_rows(step, carry):
        for slot in range(CAP):
            place = came(step, slot, 0, 3)
            square = place[0] * place[0] + place[1] * place[1] + place[2] * place[2] + 0.125
            upper = square.astype(BF16).astype(F32)
            one = jnp.ones_like(square)
            values = place + [upper, square - upper, one, one, jnp.zeros_like(square)]
            for row, value in enumerate(values):
                place_rows_ref[
                    pl.ds((slot * devices + step * 8) * 8 + row, 8, stride=8), :
                ] = value
        return carry

    lax.fori_loop(0, devices // 8, place_rows, 0)
    row = lax.broadcasted_iota(jnp.int32, (8, WIDTH), 0)

    def tile_of(base, side, number):
        slot = jnp.maximum(pairs_ref[side, number], 0)
        return base[lax.rem(slot, CAP) * devices + lax.div(slot, CAP)]

    def cube_step(step, carry):
        for part in range(CUBE_UNROLL):
            number = (step * CUBE_UNROLL + part) * 2
            lefts, rights = [], []
            for i in range(2):
                value = stacked(tile_of(place_base, 0, number + i))
                lefts += [value, value]
                last = tile_of(place_base, 1, number + i)
                turned = pltpu.roll(last, 2, 0)
                last = jnp.where(
                    row < 3, -2.0 * last, jnp.where(row < 5, 1.0, jnp.where(row < 7, turned, 0.0))
                )
                high, low = high_low(last)
                rights.append(jnp.concatenate([high, high, low, low], axis=0))
            root = lax.rsqrt(forms_of(lefts, rights))
            rows = pl.ds(pl.multiple_of(number * (WIDTH // 2), WIDTH), WIDTH)
            cubes[rows, :] = root * (root * root)
        return carry

    lax.fori_loop(0, count // (2 * CUBE_UNROLL), cube_step, 0)
    all_of(send_ref, got_ref, half, 2).wait_recv()

    def form_rows(step, carry):
        for slot in range(CAP):
            got = came(step, slot, 3, 8)
            square = got[3] * got[3] + got[4] * got[4]
            inverse = 1.0 / (1.0 + square)
            line = [2.0 * got[3] * inverse, 2.0 * got[4] * inverse, (1.0 - square) * inverse]
            for row, value in enumerate(couplings([[b * l for l in line] for b in got[:3]])):
                form_rows_ref[
                    pl.ds((slot * devices + step * 8) * ROWS + row, 8, stride=ROWS), :
                ] = value
        return carry

    lax.fori_loop(0, devices // 8, form_rows, 0)

    def fill(number, matrix):
        lefts, rights = [], []
        for i in range(2):
            high, low = high_low(tile_of(form_base, 0, number + i))
            lefts += [high, high, low]
            high, low = high_low(tile_of(form_base, 1, number + i))
            rights.append(jnp.concatenate([high, low, high], axis=0))
        rows = pl.ds(pl.multiple_of(number * (WIDTH // 2), WIDTH), WIDTH)
        high, low = high_low(forms_of(lefts, rights) * cubes[rows, :])
        matrix[pl.ds(0, WIDTH), :] = high
        matrix[pl.ds(WIDTH, WIDTH), :] = low

    def drain(number, matrix):
        value = matrix[...]
        places = [[tile_of(place_base, side, number + i) for i in range(2)] for side in range(2)]
        first, second = [[stacked(tile) for tile in side] for side in places]
        on_b = jnp.dot(
            jnp.concatenate([jnp.concatenate([p, p], axis=1) for p in first], axis=0),
            value,
            preferred_element_type=F32,
        )
        on_a = lax.dot_general(
            beside(*second), value, (((1,), (1,)), ((), ())), preferred_element_type=F32
        )
        for i in range(2):
            on_first = on_a[i * ROWS : (i + 1) * ROWS]
            on_first = on_first[:, :WIDTH] + on_first[:, WIDTH:]
            on_second = on_b[i * ROWS : (i + 1) * ROWS, i * WIDTH : (i + 1) * WIDTH]
            for side, got in enumerate((on_first, on_second)):
                force = places[side][i] * got[5:6] - (got[:8] + got[8:])
                forces[side, pl.ds(pl.multiple_of((number + i) * 8, 8), 8), :] = force

    even, odd = matrices[:UNROLL], matrices[UNROLL:]

    size = 2 * UNROLL
    halves = count // size

    def half_step(filling, filled, draining, drained):
        for part in range(UNROLL):
            if filling is not None:
                fill(filling * size + 2 * part, filled[part])
            if draining is not None:
                drain(draining * size + 2 * part, drained[part])

    def pair_step(step, carry):
        half_step(2 * step + 1, odd, 2 * step, even)
        half_step(2 * step + 2, even, 2 * step + 1, odd)
        return carry

    half_step(0, even, None, None)
    lax.fori_loop(0, halves // 2 - 1, pair_step, 0)
    half_step(halves - 1, odd, halves - 2, even)
    half_step(None, None, halves - 1, odd)
    parts = []
    for side in range(2):
        parts.append(
            jnp.concatenate(
                [
                    forces[side, pl.ds(k, count, stride=8), :]
                    for k in range(3)
                ],
                axis=1,
            )
        )
    high, low = high_low(jnp.concatenate(parts, axis=0))
    ids = jnp.concatenate([pair_rows[pl.ds(0, 1), :], pair_rows[pl.ds(1, 1), :]], axis=1)
    slots = lax.broadcasted_iota(jnp.int32, (devices, 2 * count), 0) * CAP
    for slot in range(CAP):
        chosen = jnp.where(slots + slot == ids, 1.0, 0.0).astype(BF16)
        value = jnp.dot(chosen, high, preferred_element_type=F32) + jnp.dot(
            chosen, low, preferred_element_type=F32
        )
        for k in range(3):
            out_ref[pl.ds(CAP * k + slot, devices, stride=ROWS), :] = value[
                :, k * WIDTH : (k + 1) * WIDTH
            ]

    to_chips(send_back)
    sums = gathered(total, far, over_gx)
    left = far_left(
        jnp.concatenate([sums[:, :KC], sums[:, KC:]], axis=0),
        1.0 / (math.sqrt(blocks * devices * WIDTH / KC) * math.sqrt(KC)),
    )

    def far_step(step, carry):
        for part in range(FAR_GROUPS):
            far_group(step * FAR_GROUPS + part, left, pos_ref, base_ref, o_ref, tiles[part])
        return carry

    lax.fori_loop(0, blocks // (8 * FAR_GROUPS), far_step, 0)
    rows = pl.ds(pl.multiple_of(me * ROWS, ROWS), ROWS)
    back_ref[rows, :] = out_ref[rows, :]
    all_of(send_ref, got_ref, half, 0).wait_send()
    all_of(send_ref, got_ref, half, 2).wait_send()
    done = all_of(out_ref, back_ref, BACK, 4)
    done.wait_send()
    done.wait_recv()

    back = jnp.concatenate(
        [
            jnp.concatenate(
                [back_ref[pl.ds(CAP * k + slot, devices, stride=ROWS), :] for k in range(3)], axis=1
            )
            for slot in range(CAP)
        ],
        axis=0,
    )
    high, low = high_low(back)
    ids = jnp.concatenate([id_rows[pl.ds(slot, 1), :] for slot in range(CAP)], axis=1)
    for step in range(blocks // WIDTH):
        index = lax.broadcasted_iota(jnp.int32, (WIDTH, devices * CAP), 0) + step * WIDTH
        chosen = jnp.where(index == ids, 1.0, 0.0).astype(BF16)
        rows = pl.ds(step * WIDTH, WIDTH)
        o_ref[rows, :] = (
            o_ref[rows, :]
            + jnp.dot(chosen, high, preferred_element_type=F32)
            + jnp.dot(chosen, low, preferred_element_type=F32)
        )


def far_group(step, left, pos_ref, base_ref, o_ref, tile):
    for part in range(4):
        at = (step * 8 + part * 2) * ROWS
        both = jnp.concatenate(
            [base_ref[pl.ds(pl.multiple_of(at + i * ROWS, ROWS), ROWS), :] for i in range(2)], axis=1
        )
        high, low = high_low(both)
        forms = jnp.dot(
            left, jnp.concatenate([high, low, high], axis=0), preferred_element_type=F32
        )
        root = lax.rsqrt(forms[KC:])
        weight = forms[:KC] * root * (root * root)
        w = [weight[8 * v : 8 * v + 8] for v in range(8)]
        s = [w[2 * i] + w[2 * i + 1] for i in range(4)]
        sums = [
            1.5 * (s[3] - s[0]) + 0.5 * (s[2] - s[1]),
            (w[1] + w[3]) + (w[5] + w[7]),
            (s[0] + s[1]) + (s[2] + s[3]),
        ]
        for q, value in enumerate(sums):
            for i in range(2):
                tile[pl.ds(q * 64 + (part * 2 + i) * 8, 8), :] = value[:, i * WIDTH : (i + 1) * WIDTH]
    along_x, upper, t = (
        [tile[pl.ds(q * 64 + r, 8, stride=8), :] for r in range(8)] for q in range(3)
    )
    first = (t[0] + t[1]) + (t[2] + t[3])
    second = (t[4] + t[5]) + (t[6] + t[7])
    whole = first + second
    m = [t[i] + t[i + 4] for i in range(4)]
    centers = [
        sum(along_x[1:], along_x[0]),
        2.0 * sum(upper[1:], upper[0]) - 1.5 * first - 0.5 * second,
        1.5 * (m[3] - m[0]) + 0.5 * (m[2] - m[1]),
    ]
    rows = pl.ds(pl.multiple_of(step * 8, 8), 8)
    for k in range(3):
        column = pl.ds(k * WIDTH, WIDTH)
        o_ref[rows, column] = (pos_ref[rows, column] - MIDDLE) * whole - centers[k]


VM = pl.BlockSpec(memory_space=pltpu.VMEM)


def on_device(positions, vectors, send_slots, pairs, coarse):
    size_gx, size_yz = lax.axis_size("gx"), lax.axis_size("yz")
    devices = size_gx * size_yz
    blocks, slots, count = positions.shape[0], devices * CAP, pairs.shape[0]
    ids, pair_ids = send_slots[0].T, pairs.T

    def rows(number, width=WIDTH):
        return pltpu.VMEM((number, width), F32)

    dma = pltpu.SemaphoreType.DMA
    return pl.pallas_call(
        whole_kernel,
        name="forces",
        out_shape=jax.ShapeDtypeStruct((blocks, 3 * WIDTH), F32),
        in_specs=[pl.BlockSpec(memory_space=pltpu.HBM)] * 5,
        out_specs=VM,
        scratch_shapes=[
            pltpu.SMEM((CAP, devices), jnp.int32),
            pltpu.SMEM((2, count), jnp.int32),
            pltpu.VMEM((CAP, devices), jnp.int32),
            pltpu.VMEM((2, count), jnp.int32),
            pltpu.VMEM((1, blocks), jnp.int32),
            rows(blocks, 3 * WIDTH),
            rows(blocks, 6 * WIDTH),
            pltpu.VMEM((blocks, 8, WIDTH), F32),
            rows(slots * 8),
            rows(slots * 8),
            rows(blocks * ROWS),
            rows(blocks, 9 * WIDTH),
            pltpu.VMEM((slots, 8, WIDTH), F32),
            pltpu.VMEM((slots, ROWS, WIDTH), F32),
            rows(count * WIDTH // 2, 2 * WIDTH),
            pltpu.VMEM((2, count * 8, WIDTH), F32),
            rows(devices * ROWS),
            rows(devices * ROWS),
            rows(8),
            pltpu.VMEM((size_yz, 8, WIDTH), F32),
            rows(8),
            pltpu.VMEM((size_gx, 8, WIDTH), F32),
            dma((2, LOADS)),
            dma((size_yz + size_gx,)),
            dma((size_yz + size_gx,)),
            dma((6,)),
            dma((5,)),
            pltpu.SemaphoreType.REGULAR,
        ]
        + [rows(192)] * FAR_GROUPS
        + [pltpu.VMEM((2 * WIDTH, 2 * WIDTH), BF16)] * (2 * UNROLL),
        compiler_params=pltpu.CompilerParams(
            vmem_limit_bytes=VMEM_LIMIT, collective_id=0, has_side_effects=True
        ),
    )(ids, pair_ids, coarse.reshape(1, blocks), positions, vectors)


def solution(mesh):
    placed = (
        P(("gx", "yz"), None),
        P(("gx", "yz"), None),
        P(("gx", "yz"), None, None),
        P(("gx", "yz"), None),
        P(("gx", "yz")),
    )
    return jax.shard_map(
        on_device, mesh=mesh, in_specs=placed, out_specs=P(("gx", "yz"), None), check_vma=False
    )
```

```python
import math

import jax
import jax.numpy as jnp
from jax import lax
from jax.experimental import pallas as pl
from jax.experimental.pallas import tpu as pltpu
from jax.sharding import PartitionSpec as P

MESH = pl.DeviceIdType.MESH
F32 = jnp.float32
BF16 = jnp.bfloat16
KC = 64
WIDTH = 128
MIDDLE = 2.0
ROWS = 16
UNROLL = 8
CUBE_UNROLL = 8
CAP = 4
BACK = 12
FAR_GROUPS = 4
SIDE_X = 4
LOADS = 8
VMEM_LIMIT = 54 * 2**20


def high_low(value):
    high = value.astype(BF16)
    return high, (value - high.astype(F32)).astype(BF16)


def couplings(tensor):
    scale = WIDTH**-0.25
    rows = [scale * math.sqrt(1.5) * tensor[k][k] for k in range(3)]
    for k, l in ((0, 1), (0, 2), (1, 2)):
        rows.append(scale * math.sqrt(0.75) * (tensor[k][l] + tensor[l][k]))
        rows.append(scale * 0.5 * (tensor[k][l] - tensor[l][k]))
    return rows


def features(place, tensor):
    square = place[0] * place[0] + place[1] * place[1] + place[2] * place[2] + 0.125
    upper = square.astype(BF16).astype(F32)
    one = jnp.ones_like(square)
    return couplings(tensor) + list(place) + [upper, square - upper, one, one]


def pack_group(step, pos_ref, vec_ref, base_ref, table, packed):
    rows = pl.ds(pl.multiple_of(step * 8, 8), 8)
    place = [pos_ref[rows, pl.ds(k * WIDTH, WIDTH)] - MIDDLE for k in range(3)]
    line = [vec_ref[rows, pl.ds(k * WIDTH, WIDTH)] for k in range(3)]
    burg = [vec_ref[rows, pl.ds((3 + k) * WIDTH, WIDTH)] for k in range(3)]
    for row, value in enumerate(features(place, [[b * l for l in line] for b in burg])):
        base_ref[pl.ds(step * 8 * ROWS + row, 8, stride=ROWS), :] = value
        if row < 9:
            table[rows, pl.ds(row * WIDTH, WIDTH)] = value
    square = line[0] * line[0] + line[1] * line[1] + line[2] * line[2]
    inverse = lax.rsqrt(jnp.maximum(square, 1e-36))
    side = jnp.where(line[2] < 0, -inverse, inverse)
    length = square * side
    tilt = 1.0 / (1.0 + line[2] * side)
    out = place + [b * length for b in burg] + [line[0] * side * tilt, line[1] * side * tilt]
    for row, value in enumerate(out):
        packed[pl.ds(step * 64 + row, 8, stride=8), :] = value


def cell_sums(coarse_ref, table):
    blocks = table.shape[0]
    cells = lax.broadcasted_iota(jnp.int32, (KC, blocks), 0)
    chosen = jnp.where(cells == coarse_ref[...], 1.0, 0.0).astype(BF16)
    parts = []
    for m in range(9):
        high, low = high_low(table[:, m * WIDTH : (m + 1) * WIDTH])
        parts.append(
            jnp.dot(chosen, high, preferred_element_type=F32)
            + jnp.dot(chosen, low, preferred_element_type=F32)
        )
    high, low = high_low(jnp.concatenate(parts, axis=1))
    row = lax.broadcasted_iota(jnp.int32, (ROWS, 9 * WIDTH), 0)
    lane = lax.broadcasted_iota(jnp.int32, (ROWS, 9 * WIDTH), 1)
    along = jnp.where((lane >= row * WIDTH) & (lane < row * WIDTH + WIDTH), 1.0, 0.0).astype(BF16)
    sums = [
        lax.dot_general(along, value, (((1,), (1,)), ((), ())), preferred_element_type=F32)
        for value in (high, low)
    ]
    sums = sums[0] + sums[1]
    return jnp.concatenate([sums[:8], sums[8:]], axis=1)


def far_left(sums, norm):
    row = lax.broadcasted_iota(jnp.int32, (ROWS, KC), 0)
    cell = lax.broadcasted_iota(jnp.int32, (ROWS, KC), 1)
    turned = (row == 4) | (row == 6) | (row == 8)
    square = WIDTH**-0.5
    strength = sums * jnp.where(turned, 2.0 / square * norm, norm / (1.5 * square))
    centers = [(c + (0.5 - MIDDLE)).astype(F32) for c in (cell // 16, cell // 4 % 4, cell % 4)]
    whole = centers[0] * centers[0] + centers[1] * centers[1] + centers[2] * centers[2]
    squares = jnp.where((row == 12) | (row == 13), 1.0, 0.0)
    squares = jnp.where(row == 14, whole + (1.0 - 0.125), squares)
    for k in range(3):
        squares = jnp.where(row == 9 + k, -2.0 * centers[k], squares)
    left = jnp.transpose(jnp.concatenate([strength, squares], axis=1))
    high, low = high_low(left)
    return jnp.concatenate([high, high, low], axis=1)


def stacked(tile):
    return jnp.concatenate(high_low(tile), axis=0)


def beside(first, second):
    blank = jnp.zeros_like(first)
    return jnp.concatenate(
        [jnp.concatenate([first, blank], axis=1), jnp.concatenate([blank, second], axis=1)], axis=0
    )


def forms_of(lefts, rights):
    return lax.dot_general(
        jnp.concatenate(lefts, axis=0),
        beside(*rights),
        (((0,), (0,)), ((), ())),
        preferred_element_type=F32,
    )


def whole_kernel(
    ids_hbm,
    pairs_hbm,
    coarse_hbm,
    pos_hbm,
    vec_hbm,
    o_ref,
    ids_ref,
    pairs_ref,
    id_rows,
    pair_rows,
    coarse_ref,
    pos_ref,
    vec_ref,
    packed,
    send_ref,
    got_ref,
    base_ref,
    table,
    place_base,
    form_base,
    cubes,
    forces,
    out_ref,
    back_ref,
    mine,
    near,
    total,
    far,
    load_sem,
    send_sem,
    recv_sem,
    bulk_sem,
    small_sem,
    round_sem,
    *buffers,
):
    packed_rows, place_rows_ref, form_rows_ref = [
        ref.reshape(ref.shape[0] * ref.shape[1], WIDTH) for ref in (packed, place_base, form_base)
    ]
    tiles, matrices = buffers[:FAR_GROUPS], buffers[FAR_GROUPS:]
    gx, yz = lax.axis_index("gx"), lax.axis_index("yz")
    size_gx, size_yz = lax.axis_size("gx"), lax.axis_size("yz")
    devices = size_gx * size_yz
    me = gx * size_yz + yz
    blocks = pos_ref.shape[0]
    count = pairs_ref.shape[1]
    loaded = blocks // LOADS

    def along_yz(step):
        return gx, lax.rem(yz + step, size_yz)

    def along_gx(step):
        return lax.rem(gx + step, size_gx), yz

    def loads(step):
        rows = pl.ds(pl.multiple_of(step * loaded, loaded), loaded)
        return [
            pltpu.make_async_copy(source.at[rows], target.at[rows], load_sem.at[k, step])
            for k, (source, target) in enumerate(((pos_hbm, pos_ref), (vec_hbm, vec_ref)))
        ]

    barrier = pltpu.get_barrier_semaphore()
    for turn, size in ((along_yz, size_yz), (along_gx, size_gx)):
        for step in range(1, size):
            pl.semaphore_signal(barrier, inc=1, device_id=turn(step), device_id_type=MESH)
    small = [
        pltpu.make_async_copy(source, target, small_sem.at[k])
        for k, (source, target) in enumerate(
            (
                (ids_hbm, ids_ref),
                (coarse_hbm, coarse_ref),
                (pairs_hbm, pairs_ref),
                (ids_hbm, id_rows),
                (pairs_hbm, pair_rows),
            )
        )
    ]
    for step in range(LOADS):
        for copy in loads(step):
            copy.start()
    for copy in small:
        copy.start()

    def pack(step, carry):
        for copy in loads(step):
            copy.wait()

        def group(inner, carry):
            pack_group(step * (loaded // 8) + inner, pos_ref, vec_ref, base_ref, table, packed_rows)
            return carry

        return lax.fori_loop(0, loaded // 8, group, carry)

    lax.fori_loop(0, LOADS, pack, 0)
    pl.semaphore_wait(barrier, size_yz + size_gx - 2)
    for step in range(1, size_yz):
        pl.semaphore_signal(round_sem, inc=1, device_id=along_yz(step), device_id_type=MESH)
    for copy in small:
        copy.wait()

    def exchange(source, held, turn, size, sem):
        return [
            pltpu.make_async_remote_copy(
                src_ref=source,
                dst_ref=held.at[step],
                send_sem=send_sem.at[sem + step],
                recv_sem=recv_sem.at[sem + step],
                device_id=turn(step),
                device_id_type=MESH,
            )
            for step in range(1, size)
        ]

    def gathered(source, held, copies):
        for copy in copies:
            copy.wait()
        result = source[...]
        for step in range(1, len(copies) + 1):
            result = result + held[step]
        return result

    chunk = CAP * 8
    half = chunk // 2

    def pick(device):
        for slot in range(CAP):
            source = jnp.maximum(ids_ref[slot, device], 0)
            send_ref[pl.ds(device * chunk + slot, 8, stride=CAP), :] = packed[
                source
            ]

    def bulk(to, source, target, pitch, at, size, sem):
        to_gx, to_yz = to
        device = to_gx * size_yz + to_yz
        return pltpu.make_async_remote_copy(
            src_ref=source.at[pl.ds(pl.multiple_of(device * pitch + at, 8), size)],
            dst_ref=target.at[pl.ds(pl.multiple_of(me * pitch + at, 8), size)],
            send_sem=bulk_sem.at[sem],
            recv_sem=bulk_sem.at[sem + 1],
            device_id=(to_gx, to_yz),
            device_id_type=MESH,
        )

    def all_of(source, target, size, sem):
        rows = pl.ds(0, (devices - 1) * size)
        return pltpu.make_async_remote_copy(
            src_ref=source.at[rows],
            dst_ref=target.at[rows],
            send_sem=bulk_sem.at[sem],
            recv_sem=bulk_sem.at[sem + 1],
            device_id=along_yz(1),
            device_id_type=MESH,
        )

    def to_axes(send):
        def one(turn):
            def step(number, carry):
                send(turn(number))
                return carry

            return step

        lax.fori_loop(1, size_yz, one(along_yz), 0)
        lax.fori_loop(1, size_gx, one(along_gx), 0)

    def aside(send, step):
        for part in range(size_yz - 1):
            turned = lax.rem(step + part, size_yz - 1)
            send((lax.rem(gx + step, size_gx), lax.rem(yz + 1 + turned, size_yz)))

    def to_rest(send):
        def one(step, carry):
            aside(send, step)
            return carry

        lax.fori_loop(1, size_gx, one, 0)

    side_x, side_z = SIDE_X, size_yz // 2
    side_y = size_gx // side_x
    here = (gx // side_x, lax.rem(gx, side_x), yz // 2, lax.rem(yz, 2))

    def to_chips(send):
        def turn(second, third, core, first):
            for ahead in range(first, side_y):
                y = lax.rem(here[0] + ahead, side_y)
                x = lax.rem(here[1] + ahead + second, side_x)
                z = lax.rem(here[2] + ahead + second + third, side_z)
                send((y * side_x + x, z * 2 + lax.rem(here[3] + core, 2)))

        def one(step, carry):
            turn(
                lax.rem(step, side_x),
                lax.rem(step // side_x, side_z),
                step // (side_x * side_z),
                0,
            )
            return carry

        turn(0, 0, 0, 1)
        lax.fori_loop(1, 2 * side_x * side_z, one, 0)

    def send_first(to):
        pick(to[0] * size_yz + to[1])
        bulk(to, send_ref, got_ref, chunk, 0, half, 0).start()

    def send_second(to):
        bulk(to, send_ref, got_ref, chunk, half, half, 2).start()

    def send_back(to):
        bulk(to, out_ref, back_ref, ROWS, 0, BACK, 4).start()

    to_axes(send_first)
    mine[...] = cell_sums(coarse_ref, table)
    over_yz = exchange(mine, near, along_yz, size_yz, 0)
    over_gx = exchange(total, far, along_gx, size_gx, size_yz)
    for copy in over_yz:
        copy.start()
    pl.semaphore_wait(round_sem, size_yz - 1)
    to_rest(send_first)
    to_chips(send_second)
    total[...] = gathered(mine, near, over_yz)
    for copy in over_gx:
        copy.start()
    pick(me)
    rows = pl.ds(pl.multiple_of(me * chunk, chunk), chunk)
    got_ref[rows, :] = send_ref[rows, :]
    form_base[...] = jnp.zeros_like(form_base)

    def came(step, slot, first, last):
        return [
            got_ref[pl.ds(step * 8 * chunk + CAP * k + slot, 8, stride=chunk), :]
            for k in range(first, last)
        ]

    all_of(send_ref, got_ref, half, 0).wait_recv()

    def place_rows(step, carry):
        for slot in range(CAP):
            place = came(step, slot, 0, 3)
            square = place[0] * place[0] + place[1] * place[1] + place[2] * place[2] + 0.125
            upper = square.astype(BF16).astype(F32)
            one = jnp.ones_like(square)
            values = place + [upper, square - upper, one, one, jnp.zeros_like(square)]
            for row, value in enumerate(values):
                place_rows_ref[
                    pl.ds((slot * devices + step * 8) * 8 + row, 8, stride=8), :
                ] = value
        return carry

    lax.fori_loop(0, devices // 8, place_rows, 0)
    row = lax.broadcasted_iota(jnp.int32, (8, WIDTH), 0)

    def tile_of(base, side, number):
        slot = jnp.maximum(pairs_ref[side, number], 0)
        return base[lax.rem(slot, CAP) * devices + lax.div(slot, CAP)]

    def cube_step(step, carry):
        for part in range(CUBE_UNROLL):
            number = (step * CUBE_UNROLL + part) * 2
            lefts, rights = [], []
            for i in range(2):
                value = stacked(tile_of(place_base, 0, number + i))
                lefts += [value, value]
                last = tile_of(place_base, 1, number + i)
                turned = pltpu.roll(last, 2, 0)
                last = jnp.where(
                    row < 3, -2.0 * last, jnp.where(row < 5, 1.0, jnp.where(row < 7, turned, 0.0))
                )
                high, low = high_low(last)
                rights.append(jnp.concatenate([high, high, low, low], axis=0))
            root = lax.rsqrt(forms_of(lefts, rights))
            rows = pl.ds(pl.multiple_of(number * (WIDTH // 2), WIDTH), WIDTH)
            cubes[rows, :] = root * (root * root)
        return carry

    lax.fori_loop(0, count // (2 * CUBE_UNROLL), cube_step, 0)
    all_of(send_ref, got_ref, half, 2).wait_recv()

    def form_rows(step, carry):
        for slot in range(CAP):
            got = came(step, slot, 3, 8)
            square = got[3] * got[3] + got[4] * got[4]
            inverse = 1.0 / (1.0 + square)
            line = [2.0 * got[3] * inverse, 2.0 * got[4] * inverse, (1.0 - square) * inverse]
            for row, value in enumerate(couplings([[b * l for l in line] for b in got[:3]])):
                form_rows_ref[
                    pl.ds((slot * devices + step * 8) * ROWS + row, 8, stride=ROWS), :
                ] = value
        return carry

    lax.fori_loop(0, devices // 8, form_rows, 0)

    def fill(number, matrix):
        lefts, rights = [], []
        for i in range(2):
            high, low = high_low(tile_of(form_base, 0, number + i))
            lefts += [high, high, low]
            high, low = high_low(tile_of(form_base, 1, number + i))
            rights.append(jnp.concatenate([high, low, high], axis=0))
        rows = pl.ds(pl.multiple_of(number * (WIDTH // 2), WIDTH), WIDTH)
        high, low = high_low(forms_of(lefts, rights) * cubes[rows, :])
        matrix[pl.ds(0, WIDTH), :] = high
        matrix[pl.ds(WIDTH, WIDTH), :] = low

    def drain(number, matrix):
        value = matrix[...]
        places = [[tile_of(place_base, side, number + i) for i in range(2)] for side in range(2)]
        first, second = [[stacked(tile) for tile in side] for side in places]
        on_b = jnp.dot(
            jnp.concatenate([jnp.concatenate([p, p], axis=1) for p in first], axis=0),
            value,
            preferred_element_type=F32,
        )
        on_a = lax.dot_general(
            beside(*second), value, (((1,), (1,)), ((), ())), preferred_element_type=F32
        )
        for i in range(2):
            on_first = on_a[i * ROWS : (i + 1) * ROWS]
            on_first = on_first[:, :WIDTH] + on_first[:, WIDTH:]
            on_second = on_b[i * ROWS : (i + 1) * ROWS, i * WIDTH : (i + 1) * WIDTH]
            for side, got in enumerate((on_first, on_second)):
                force = places[side][i] * got[5:6] - (got[:8] + got[8:])
                forces[side, pl.ds(pl.multiple_of((number + i) * 8, 8), 8), :] = force

    even, odd = matrices[:UNROLL], matrices[UNROLL:]

    size = 2 * UNROLL
    halves = count // size

    def half_step(filling, filled, draining, drained):
        for part in range(UNROLL):
            if filling is not None:
                fill(filling * size + 2 * part, filled[part])
            if draining is not None:
                drain(draining * size + 2 * part, drained[part])

    def pair_step(step, carry):
        half_step(2 * step + 1, odd, 2 * step, even)
        half_step(2 * step + 2, even, 2 * step + 1, odd)
        return carry

    half_step(0, even, None, None)
    lax.fori_loop(0, halves // 2 - 1, pair_step, 0)
    half_step(halves - 1, odd, halves - 2, even)
    half_step(None, None, halves - 1, odd)
    parts = []
    for side in range(2):
        parts.append(
            jnp.concatenate(
                [
                    forces[side, pl.ds(k, count, stride=8), :]
                    for k in range(3)
                ],
                axis=1,
            )
        )
    high, low = high_low(jnp.concatenate(parts, axis=0))
    ids = jnp.concatenate([pair_rows[pl.ds(0, 1), :], pair_rows[pl.ds(1, 1), :]], axis=1)
    slots = lax.broadcasted_iota(jnp.int32, (devices, 2 * count), 0) * CAP
    for slot in range(CAP):
        chosen = jnp.where(slots + slot == ids, 1.0, 0.0).astype(BF16)
        value = jnp.dot(chosen, high, preferred_element_type=F32) + jnp.dot(
            chosen, low, preferred_element_type=F32
        )
        for k in range(3):
            out_ref[pl.ds(CAP * k + slot, devices, stride=ROWS), :] = value[
                :, k * WIDTH : (k + 1) * WIDTH
            ]

    to_chips(send_back)
    sums = gathered(total, far, over_gx)
    left = far_left(
        jnp.concatenate([sums[:, :KC], sums[:, KC:]], axis=0),
        1.0 / (math.sqrt(blocks * devices * WIDTH / KC) * math.sqrt(KC)),
    )

    def far_step(step, carry):
        for part in range(FAR_GROUPS):
            far_group(step * FAR_GROUPS + part, left, pos_ref, base_ref, o_ref, tiles[part])
        return carry

    lax.fori_loop(0, blocks // (8 * FAR_GROUPS), far_step, 0)
    rows = pl.ds(pl.multiple_of(me * ROWS, ROWS), ROWS)
    back_ref[rows, :] = out_ref[rows, :]
    all_of(send_ref, got_ref, half, 0).wait_send()
    all_of(send_ref, got_ref, half, 2).wait_send()
    done = all_of(out_ref, back_ref, BACK, 4)
    done.wait_send()
    done.wait_recv()

    back = jnp.concatenate(
        [
            jnp.concatenate(
                [back_ref[pl.ds(CAP * k + slot, devices, stride=ROWS), :] for k in range(3)], axis=1
            )
            for slot in range(CAP)
        ],
        axis=0,
    )
    high, low = high_low(back)
    ids = jnp.concatenate([id_rows[pl.ds(slot, 1), :] for slot in range(CAP)], axis=1)
    for step in range(blocks // WIDTH):
        index = lax.broadcasted_iota(jnp.int32, (WIDTH, devices * CAP), 0) + step * WIDTH
        chosen = jnp.where(index == ids, 1.0, 0.0).astype(BF16)
        rows = pl.ds(step * WIDTH, WIDTH)
        o_ref[rows, :] = (
            o_ref[rows, :]
            + jnp.dot(chosen, high, preferred_element_type=F32)
            + jnp.dot(chosen, low, preferred_element_type=F32)
        )


def far_group(step, left, pos_ref, base_ref, o_ref, tile):
    for part in range(4):
        at = (step * 8 + part * 2) * ROWS
        both = jnp.concatenate(
            [base_ref[pl.ds(pl.multiple_of(at + i * ROWS, ROWS), ROWS), :] for i in range(2)], axis=1
        )
        high, low = high_low(both)
        forms = jnp.dot(
            left, jnp.concatenate([high, low, high], axis=0), preferred_element_type=F32
        )
        root = lax.rsqrt(forms[KC:])
        weight = forms[:KC] * root * (root * root)
        w = [weight[8 * v : 8 * v + 8] for v in range(8)]
        s = [w[2 * i] + w[2 * i + 1] for i in range(4)]
        sums = [
            1.5 * (s[3] - s[0]) + 0.5 * (s[2] - s[1]),
            (w[1] + w[3]) + (w[5] + w[7]),
            (s[0] + s[1]) + (s[2] + s[3]),
        ]
        for q, value in enumerate(sums):
            for i in range(2):
                tile[pl.ds(q * 64 + (part * 2 + i) * 8, 8), :] = value[:, i * WIDTH : (i + 1) * WIDTH]
    along_x, upper, t = (
        [tile[pl.ds(q * 64 + r, 8, stride=8), :] for r in range(8)] for q in range(3)
    )
    first = (t[0] + t[1]) + (t[2] + t[3])
    second = (t[4] + t[5]) + (t[6] + t[7])
    whole = first + second
    m = [t[i] + t[i + 4] for i in range(4)]
    centers = [
        sum(along_x[1:], along_x[0]),
        2.0 * sum(upper[1:], upper[0]) - 1.5 * first - 0.5 * second,
        1.5 * (m[3] - m[0]) + 0.5 * (m[2] - m[1]),
    ]
    rows = pl.ds(pl.multiple_of(step * 8, 8), 8)
    for k in range(3):
        column = pl.ds(k * WIDTH, WIDTH)
        o_ref[rows, column] = (pos_ref[rows, column] - MIDDLE) * whole - centers[k]


VM = pl.BlockSpec(memory_space=pltpu.VMEM)


def on_device(positions, vectors, send_slots, pairs, coarse):
    size_gx, size_yz = lax.axis_size("gx"), lax.axis_size("yz")
    devices = size_gx * size_yz
    blocks, slots, count = positions.shape[0], devices * CAP, pairs.shape[0]
    ids, pair_ids = send_slots[0].T, pairs.T

    def rows(number, width=WIDTH):
        return pltpu.VMEM((number, width), F32)

    dma = pltpu.SemaphoreType.DMA
    return pl.pallas_call(
        whole_kernel,
        name="forces",
        out_shape=jax.ShapeDtypeStruct((blocks, 3 * WIDTH), F32),
        in_specs=[pl.BlockSpec(memory_space=pltpu.HBM)] * 5,
        out_specs=VM,
        scratch_shapes=[
            pltpu.SMEM((CAP, devices), jnp.int32),
            pltpu.SMEM((2, count), jnp.int32),
            pltpu.VMEM((CAP, devices), jnp.int32),
            pltpu.VMEM((2, count), jnp.int32),
            pltpu.VMEM((1, blocks), jnp.int32),
            rows(blocks, 3 * WIDTH),
            rows(blocks, 6 * WIDTH),
            pltpu.VMEM((blocks, 8, WIDTH), F32),
            rows(slots * 8),
            rows(slots * 8),
            rows(blocks * ROWS),
            rows(blocks, 9 * WIDTH),
            pltpu.VMEM((slots, 8, WIDTH), F32),
            pltpu.VMEM((slots, ROWS, WIDTH), F32),
            rows(count * WIDTH // 2, 2 * WIDTH),
            pltpu.VMEM((2, count * 8, WIDTH), F32),
            rows(devices * ROWS),
            rows(devices * ROWS),
            rows(8),
            pltpu.VMEM((size_yz, 8, WIDTH), F32),
            rows(8),
            pltpu.VMEM((size_gx, 8, WIDTH), F32),
            dma((2, LOADS)),
            dma((size_yz + size_gx,)),
            dma((size_yz + size_gx,)),
            dma((6,)),
            dma((5,)),
            pltpu.SemaphoreType.REGULAR,
        ]
        + [rows(192)] * FAR_GROUPS
        + [pltpu.VMEM((2 * WIDTH, 2 * WIDTH), BF16)] * (2 * UNROLL),
        compiler_params=pltpu.CompilerParams(
            vmem_limit_bytes=VMEM_LIMIT, collective_id=0, has_side_effects=True
        ),
    )(ids, pair_ids, coarse.reshape(1, blocks), positions, vectors)


def solution(mesh):
    placed = (
        P(("gx", "yz"), None),
        P(("gx", "yz"), None),
        P(("gx", "yz"), None, None),
        P(("gx", "yz"), None),
        P(("gx", "yz")),
    )
    return jax.shard_map(
        on_device, mesh=mesh, in_specs=placed, out_specs=P(("gx", "yz"), None), check_vma=False
    )
```
